512 devices in a mesh: seq: 32 (over z, x), tp: 16 (over y, core).
Axes of the slice: x: 4, y: 8, z: 8, core: 2. Of those that a mesh axis runs over, the one named last changes fastest.
Arguments:
- residual_in: bfloat16 [8192, 8192], P('seq', 'tp'), may hold values from -6 to 6
- features: bfloat16 [3, 8192, 8192], P(None, 'seq', 'tp'), may hold values from -6 to 6
- short_mr: float32 [3, 7, 8192], P(None, None, 'tp'), may hold values from -2 to 2
- medium: bfloat16 [128, 512], P(None, 'tp'), may hold values from -0.5 to 0.5
- skip_mr: float32 [8192], P('tp'), may hold values from 0.5 to 1.5
- li_gates: bfloat16 [2, 8192, 8192], P(None, 'seq', 'tp'), may hold values from -6 to 6
- short_li: float32 [3, 7, 8192], P(None, None, 'tp'), may hold values from -2 to 2
- poles: float32 [16, 8192], P(None, 'tp'), may hold values from 0 to 1, as said below
- residues: float32 [16, 8192], P(None, 'tp'), may hold values from -0.5 to 0.5
- skip_li: float32 [8192], P('tp'), may hold values from 0.5 to 1.5
- w_out: bfloat16 [8192, 8192], P('seq', 'tp'), may hold values from -0.0625 to 0.0625
Outputs:
- block_out: bfloat16 [8192, 8192], P('seq', 'tp')
The draws below stay inside these ranges and needn't reach their ends.
Inputs may be any that keep to these rules, and one draw needn't show every extreme that they name: `poles`: every pole lies strictly between 0 and 1.
All inputs are finite; a program needn't handle non-finite values.
Results may differ from the reference program's by a relative error of at most 0.0064.
Values may be sent and summed in bfloat16 or wider, within the bound.
No kernel may reach another device: no remote copies, remote signals or barrier semaphores. Data moves between devices by JAX's collectives and lax.ppermute only.
A program may use at most 128 MiB of HBM per device.

```python
import math
import jax
import jax.numpy as jnp
from jax import lax

D = 8192
MODES = 16
SHORT_TAPS = 7
MED_TAPS = 128
GROUPS = 512
TOKENS = 8192


def mode_rates(key):
    uniform_draw = jax.random.uniform(jax.random.fold_in(key, 101), (MODES, D), jnp.float32)
    slow_rate = math.log(10.0) / TOKENS
    fast_rate = 1.0 / 30.0
    lowest = math.log(slow_rate * slow_rate / fast_rate)
    return jnp.exp(lowest + uniform_draw * (math.log(fast_rate) - lowest))


def draw_poles(key, part):
    return jnp.exp(-mode_rates(key))


def draw_residues(key, part):
    rates = mode_rates(key)
    normal_draw = jax.random.truncated_normal(jax.random.fold_in(key, 103), -4.0, 4.0, (MODES, D), jnp.float32)
    return normal_draw * jnp.sqrt(2.0 * rates + 2.0 / TOKENS) * 0.25


def block_scale(stream_key, dims, split, smallest, top_value):
    loudness = 1.0
    for position, shards_of in split:
        heights = jax.random.uniform(jax.random.fold_in(jax.random.fold_in(stream_key, 6), position), (shards_of,), jnp.float32, smallest / len(split), top_value / len(split))
        loudness = loudness * jnp.repeat(jnp.exp(heights), dims[position] // shards_of).reshape((-1,) + (1,) * (len(dims) - 1 - position))
    return loudness


def normal_values(rng, dims, scale, most, cuts=(), kind=jnp.bfloat16):
    level = block_scale(rng, dims, cuts, -0.22, 0.18) if cuts else 1.0
    values = jax.random.normal(rng, dims, jnp.float32) * scale * level
    return jnp.minimum(jnp.maximum(values, -most), most).astype(kind)


def setup_inputs(seed: int = 0) -> dict:
    key_of = jax.random.split(jax.random.key(seed), 12)
    residual_in = normal_values(key_of[0], (TOKENS, D), 1.0, 6.0, ((0, 32), (1, 16)))
    features = normal_values(key_of[1], (3, TOKENS, D), 1.0, 6.0, ((1, 32), (2, 16)))
    short_mr = normal_values(key_of[2], (3, SHORT_TAPS, D), 0.4, 2.0, ((2, 16),), jnp.float32)
    medium = normal_values(key_of[3], (MED_TAPS, GROUPS), MED_TAPS ** -0.5, 0.5, ((1, 16),))
    skip_mr = jnp.clip(1.0 + 0.1 * jax.random.normal(key_of[4], (D,), jnp.float32), 0.5, 1.5)
    li_gates = normal_values(key_of[5], (2, TOKENS, D), 1.0, 6.0, ((1, 32), (2, 16)))
    short_li = normal_values(key_of[6], (3, SHORT_TAPS, D), 0.4, 2.0, ((2, 16),), jnp.float32)
    poles = draw_poles(jax.random.fold_in(key_of[11], 71), 0)
    residues = draw_residues(jax.random.fold_in(key_of[11], 71), 0)
    skip_li = jnp.clip(1.0 + 0.1 * jax.random.normal(key_of[9], (D,), jnp.float32), 0.5, 1.5)
    w_out = normal_values(key_of[10], (D, D), D ** -0.5, 0.0625, ((0, 32), (1, 16)))
    return dict(residual_in=residual_in, features=features, short_mr=short_mr, medium=medium, skip_mr=skip_mr, li_gates=li_gates, short_li=short_li, poles=poles, residues=residues, skip_li=skip_li, w_out=w_out)


block_len = 32
highest = lax.Precision.HIGHEST


def short_conv(extended, tap_table):
    rim_rows = tap_table.shape[1] - 1
    tok_rows = extended.shape[1] - rim_rows
    running = jnp.zeros((extended.shape[0], tok_rows, extended.shape[2]), jnp.float32)
    for tap_lag in range(tap_table.shape[1]):
        window = extended[:, rim_rows - tap_lag: rim_rows - tap_lag + tok_rows].astype(jnp.float32)
        running = running + tap_table[:, tap_lag][:, None, :] * window
    return running


def medium_bands(tap_table):
    length = tap_table.shape[0]
    groups = tap_table.shape[1]
    zero_rows = jnp.zeros((length - 1, groups), tap_table.dtype)
    tap_line = jnp.concatenate([zero_rows, tap_table[::-1], zero_rows], axis=0)
    bands = jnp.stack([tap_line[length - 1 - row: 3 * length - 2 - row] for row in range(length)])
    band_head = bands[:, :length]
    band_tail = jnp.concatenate([bands[:, length:], jnp.zeros((length, 1, groups), tap_table.dtype)], axis=1)
    return band_head, band_tail


def medium_conv(extended, tap_table):
    length = tap_table.shape[0]
    tok_rows = extended.shape[0] - (length - 1)
    channels = extended.shape[1]
    groups = tap_table.shape[1]
    group_width = channels // groups
    band_head, band_tail = medium_bands(tap_table)
    padded = jnp.concatenate([extended, jnp.zeros((1, channels), extended.dtype)], axis=0)
    blocks = tok_rows // length
    win_head = padded[:tok_rows].reshape(blocks, length, groups, group_width).astype(jnp.float32)
    win_tail = padded[length:tok_rows + length].reshape(blocks, length, groups, group_width).astype(jnp.float32)
    result = jnp.einsum('ijg,bjgw->bigw', band_head.astype(jnp.float32), win_head, precision=highest)
    result = result + jnp.einsum('ijg,bjgw->bigw', band_tail.astype(jnp.float32), win_tail, precision=highest)
    return result.reshape(tok_rows, channels)


def long_local(z_two, poles, residues):
    tok_rows, channels = z_two.shape
    blocks = tok_rows // block_len
    log_poles = jnp.log(poles)
    lag_steps = jnp.arange(block_len + 1).astype(jnp.float32)
    powers = jnp.exp(lag_steps[:, None, None] * log_poles[None])
    filter_taps = jnp.sum(residues[None] * powers[:block_len], axis=1)
    flipped = jnp.concatenate([filter_taps[::-1], jnp.zeros((block_len - 1, channels), jnp.float32)], axis=0)
    toeplitz = jnp.stack([flipped[block_len - 1 - row: 2 * block_len - 1 - row] for row in range(block_len)])
    pieces = z_two.reshape(blocks, block_len, channels)
    inside = jnp.einsum('ijc,njc->nic', toeplitz, pieces, precision=highest)
    block_ends = jnp.einsum('jmc,njc->nmc', powers[block_len - 1::-1], pieces, precision=highest)
    lam_block = powers[block_len]

    def advance(carried_state, block_end):
        return lam_block * carried_state + block_end, carried_state

    state_end, starts = lax.scan(advance, jnp.zeros_like(lam_block), block_ends)
    mode_gain = residues[None] * powers[1:]
    across = jnp.einsum('imc,nmc->nic', mode_gain, starts, precision=highest)
    return (inside + across).reshape(tok_rows, channels), state_end, mode_gain, log_poles


def reference(residual_in, features, short_mr, medium, skip_mr, li_gates, short_li, poles, residues, skip_li, w_out):
    rim_rows = short_mr.shape[1] - 1
    med_reach = medium.shape[0] - 1
    channels = features.shape[2]
    mr_streams = short_conv(jnp.concatenate([jnp.zeros((3, rim_rows, channels), jnp.bfloat16), features], axis=1), short_mr)
    z_one = (mr_streams[1] * mr_streams[2]).astype(jnp.bfloat16)
    medium_out = medium_conv(jnp.concatenate([jnp.zeros((med_reach, channels), jnp.bfloat16), z_one], axis=0), medium)
    y_one = (mr_streams[0] * (medium_out + skip_mr * z_one.astype(jnp.float32))).astype(jnp.bfloat16)
    li_inputs = jnp.concatenate([li_gates, y_one[None]], axis=0)
    li_streams = short_conv(jnp.concatenate([jnp.zeros((3, rim_rows, channels), jnp.bfloat16), li_inputs], axis=1), short_li)
    z_two = li_streams[1] * li_streams[2]
    long_out = long_local(z_two, poles, residues)[0]
    y_two = (li_streams[0] * (long_out + skip_li * z_two)).astype(jnp.bfloat16)
    projected = jnp.dot(y_two, w_out, preferred_element_type=jnp.float32)
    return (residual_in.astype(jnp.float32) + projected).astype(jnp.bfloat16)
```

```python
import jax
import jax.numpy as jnp
from jax import lax
from jax.experimental import pallas as pl
from jax.experimental.pallas import tpu as pltpu
from jax.sharding import PartitionSpec as P

f32 = jnp.float32
bf16 = jnp.bfloat16
LANES = 128
SEGMENTS = 8
FRONT = 144
REACH = 16


def small(mebibytes):
    return pltpu.CompilerParams(vmem_limit_bytes=int(mebibytes * 1024) * 1024)


def power(base, exponent):
    result, square = None, base
    while exponent:
        if exponent & 1:
            result = square if result is None else result * square
        exponent >>= 1
        if exponent:
            square = square * square
    return result


def bands_kernel(line_ref, out_ref):
    for group in range(out_ref.shape[0]):
        rows = jnp.broadcast_to(line_ref[group : group + 1, :], out_ref.shape[1:])
        out_ref[group] = pltpu.roll(rows, 0, 1, stride=1, stride_axis=0).astype(bf16)


def make_bands(medium):
    taps, groups = medium.shape
    line = jnp.concatenate(
        [jnp.zeros((1, groups), medium.dtype), medium[::-1], jnp.zeros((taps - 1, groups), medium.dtype)]
    )
    per_step = 8
    return pl.pallas_call(
        bands_kernel,
        grid=(groups // per_step,),
        in_specs=[pl.BlockSpec((per_step, 2 * taps), lambda i: (i, 0))],
        out_specs=pl.BlockSpec((per_step, taps, 2 * taps), lambda i: (i, 0, 0)),
        out_shape=jax.ShapeDtypeStruct((groups, taps, 2 * taps), bf16),
        compiler_params=small(8),
        name="bands",
    )(line.T.astype(f32))


def conv_rows(buffer, taps, first, count):
    total = None
    for lag in range(len(taps)):
        term = taps[lag] * buffer[pl.ds(first - lag, count), :]
        total = term if total is None else total + term
    return total


def mix_kernel(
    feat_ref, gate_ref, halo_ref, short_mr_ref, short_li_ref, skip_ref, band_ref, pole_ref,
    z_ref, q_ref, seg_ref, end_ref,
    k_buf, v_buf, s_buf, y_buf, zwin, state_buf, med_buf,
):
    tok_rows = feat_ref.shape[1]
    taps_med = band_ref.shape[1]
    groups = band_ref.shape[0]
    group_width = LANES // groups
    n_short = short_mr_ref.shape[1]
    step = 32

    def taps_of(ref, stream):
        return [ref[stream, lag : lag + 1, :] for lag in range(n_short)]

    for buf, at, stream in ((k_buf, 0, 1), (v_buf, FRONT, 2)):
        buf[0:8, :] = jnp.zeros((8, LANES), f32)
        buf[8 : 8 + FRONT, :] = halo_ref[at : at + FRONT, :].astype(f32)
        buf[8 + FRONT :, :] = feat_ref[stream].astype(f32)
    k_taps, v_taps = taps_of(short_mr_ref, 1), taps_of(short_mr_ref, 2)
    lead = 2 * taps_med - FRONT
    zwin[0:lead, :] = jnp.zeros((lead, LANES), bf16)
    for first in range(0, FRONT + tok_rows, 16):
        count = 16
        k_part = conv_rows(k_buf, k_taps, 8 + first, count)
        v_part = conv_rows(v_buf, v_taps, 8 + first, count)
        zwin[lead + first : lead + first + count, :] = (k_part * v_part).astype(bf16)

    owner = lax.broadcasted_iota(jnp.int32, (8, LANES), 1) // group_width
    masks = [owner == group for group in range(groups)]

    def pick(product, rows, start):
        for r in range(0, rows, 8):
            total = product[r : r + 8]
            for group in range(1, groups):
                total = jnp.where(masks[group], product[group * rows + r : group * rows + r + 8], total)
            med_buf[start + r : start + r + 8, :] = total

    tail = band_ref[:, taps_med - 16 :, :].reshape(groups * 16, 2 * taps_med)
    pick(jnp.dot(tail, zwin[0 : 2 * taps_med, :], preferred_element_type=f32), 16, 0)
    whole = band_ref[...].reshape(groups * taps_med, 2 * taps_med)
    for block in range(tok_rows // taps_med):
        window = zwin[taps_med * (block + 1) : taps_med * (block + 3), :]
        pick(jnp.dot(whole, window, preferred_element_type=f32), taps_med, 16 + taps_med * block)

    s_buf[0:16, :] = halo_ref[2 * FRONT : 2 * FRONT + 16, :].astype(f32)
    s_buf[16:, :] = feat_ref[0].astype(f32)
    q_taps = taps_of(short_mr_ref, 0)
    skip = skip_ref[...]
    z_last = 2 * taps_med
    q_part = conv_rows(s_buf, q_taps, 8, 8)
    z_part = zwin[z_last - 16 : z_last, :].astype(f32)[8:16]
    y_buf[0:8, :] = (q_part * (med_buf[8:16, :] + skip * z_part)).astype(bf16).astype(f32)
    for first in range(0, tok_rows, step):
        q_part = conv_rows(s_buf, q_taps, 16 + first, step)
        z_part = zwin[z_last + first : z_last + first + step, :].astype(f32)
        y_part = q_part * (med_buf[16 + first : 16 + first + step, :] + skip * z_part)
        y_buf[8 + first : 8 + first + step, :] = y_part.astype(bf16).astype(f32)

    for buf, at, stream in ((k_buf, 16, 0), (v_buf, 32, 1)):
        tail_rows = halo_ref[2 * FRONT + at : 2 * FRONT + at + 16, :].astype(f32)
        buf[0:8, :] = tail_rows[8:16]
        buf[8 : 8 + tok_rows, :] = gate_ref[stream].astype(f32)
    li_taps = [taps_of(short_li_ref, i) for i in range(3)]
    for first in range(0, tok_rows, step):
        rows = slice(first, first + step)
        q_ref[rows, :] = conv_rows(k_buf, li_taps[0], 8 + first, step)
        k_part = conv_rows(v_buf, li_taps[1], 8 + first, step)
        z_ref[rows, :] = k_part * conv_rows(y_buf, li_taps[2], 8 + first, step)

    modes = pole_ref.shape[0]
    seg_rows = tok_rows // SEGMENTS
    pole = [jnp.broadcast_to(pole_ref[m : m + 1, :], (SEGMENTS, LANES)) for m in range(modes)]
    state = [None] * modes
    for t in range(seg_rows):
        z_now = z_ref[pl.ds(t, SEGMENTS, stride=seg_rows), :]
        state = [z_now if s is None else pole[m] * s + z_now for m, s in enumerate(state)]
    for m in range(modes):
        state_buf[m * SEGMENTS : (m + 1) * SEGMENTS, :] = state[m]
    seg_decay = power(pole_ref[...], seg_rows)
    total = state_buf[pl.ds(0, modes, stride=SEGMENTS), :]
    for s in range(1, SEGMENTS):
        total = seg_decay * total + state_buf[pl.ds(s, modes, stride=SEGMENTS), :]
    seg_ref[...] = state_buf[...]
    for copy in range(end_ref.shape[0]):
        end_ref[copy] = total


def mix(features, gates, halo, short_mr, short_li, skip_mr, bands, poles, copies):
    tok_rows, channels = features.shape[1:]
    modes = poles.shape[0]
    groups = bands.shape[0]
    tiles = channels // LANES
    per_tile = groups // tiles
    taps_med = bands.shape[1]
    shapes = [
        ((tok_rows, channels), (tok_rows, LANES), lambda i: (0, i)),
        ((tok_rows, channels), (tok_rows, LANES), lambda i: (0, i)),
        ((modes * SEGMENTS, channels), (modes * SEGMENTS, LANES), lambda i: (0, i)),
        ((copies, modes, channels), (copies, modes, LANES), lambda i: (0, 0, i)),
    ]
    return pl.pallas_call(
        mix_kernel,
        grid=(tiles,),
        in_specs=[
            pl.BlockSpec((3, tok_rows, LANES), lambda i: (0, 0, i)),
            pl.BlockSpec((2, tok_rows, LANES), lambda i: (0, 0, i)),
            pl.BlockSpec((halo.shape[0], LANES), lambda i: (0, i)),
            pl.BlockSpec((3, short_mr.shape[1], LANES), lambda i: (0, 0, i)),
            pl.BlockSpec((3, short_li.shape[1], LANES), lambda i: (0, 0, i)),
            pl.BlockSpec((1, LANES), lambda i: (0, i)),
            pl.BlockSpec((per_tile, taps_med, 2 * taps_med), lambda i: (i, 0, 0)),
            pl.BlockSpec((modes, LANES), lambda i: (0, i)),
        ],
        out_specs=[pl.BlockSpec(block, index) for _, block, index in shapes],
        out_shape=[pltpu.HBM(shape, f32) for shape, _, _ in shapes],
        scratch_shapes=[
            pltpu.VMEM((8 + FRONT + tok_rows, LANES), f32),
            pltpu.VMEM((8 + FRONT + tok_rows, LANES), f32),
            pltpu.VMEM((16 + tok_rows, LANES), f32),
            pltpu.VMEM((8 + tok_rows, LANES), f32),
            pltpu.VMEM((2 * taps_med + tok_rows, LANES), bf16),
            pltpu.VMEM((modes * SEGMENTS, LANES), f32),
            pltpu.VMEM((16 + tok_rows, LANES), f32),
        ],
        compiler_params=small(16),
        name="mix",
    )(features, gates, halo, short_mr, short_li, skip_mr.reshape(1, channels), bands, poles)


def near_kernel(tok_rows, place_ref, ends_ref, pole_ref, part_ref, total_ref):
    mine = place_ref[1]
    decay = power(pole_ref[...], tok_rows)
    part = jnp.zeros(decay.shape, f32)
    total = jnp.zeros(decay.shape, f32)
    for other in range(ends_ref.shape[0]):
        end = ends_ref[other]
        part = jnp.where(other < mine, decay * part + end, part)
        total = decay * total + end
    part_ref[...] = part
    for copy in range(total_ref.shape[0]):
        total_ref[copy] = total


def near(place, ends, poles, tok_rows, copies):
    return pl.pallas_call(
        lambda *refs: near_kernel(tok_rows, *refs),
        in_specs=[
            pl.BlockSpec(memory_space=pltpu.SMEM),
            pl.BlockSpec(memory_space=pltpu.VMEM),
            pl.BlockSpec(memory_space=pltpu.VMEM),
        ],
        out_shape=[
            jax.ShapeDtypeStruct(poles.shape, f32),
            jax.ShapeDtypeStruct((copies, *poles.shape), f32),
        ],
        compiler_params=small(4),
        name="near",
    )(place, ends, poles)


def close_kernel(
    near_count, place_ref, z_ref, q_ref, seg_ref, part_ref, total_ref, pole_ref, res_ref, skip_ref,
    y_ref, state_buf, out_buf,
):
    tok_rows = z_ref.shape[0]
    modes = pole_ref.shape[0]
    seg_rows = tok_rows // SEGMENTS
    row, mine = place_ref[0], place_ref[1]
    seg_decay = power(pole_ref[...], seg_rows)
    decay = power(seg_decay, SEGMENTS)
    row_decay = power(decay, near_count)
    far = jnp.zeros(decay.shape, f32)
    for other in range(total_ref.shape[0]):
        far = jnp.where(other < row, row_decay * far + total_ref[other], far)
    for step in range(near_count - 1):
        far = jnp.where(step < mine, decay * far, far)
    start = far + part_ref[...]
    for s in range(SEGMENTS):
        state_buf[pl.ds(s, modes, stride=SEGMENTS), :] = start
        if s < SEGMENTS - 1:
            start = seg_decay * start + seg_ref[pl.ds(s, modes, stride=SEGMENTS), :]
    state = [state_buf[m * SEGMENTS : (m + 1) * SEGMENTS, :] for m in range(modes)]
    pole = [jnp.broadcast_to(pole_ref[m : m + 1, :], (SEGMENTS, LANES)) for m in range(modes)]
    gain = [jnp.broadcast_to(res_ref[m : m + 1, :], (SEGMENTS, LANES)) for m in range(modes)]
    skip = jnp.broadcast_to(skip_ref[...], (SEGMENTS, LANES))
    for t in range(seg_rows):
        rows = pl.ds(t, SEGMENTS, stride=seg_rows)
        z_now = z_ref[rows, :]
        sums = [skip * z_now, None, None, None]
        for m in range(modes):
            state[m] = pole[m] * state[m] + z_now
            term = gain[m] * state[m]
            sums[m % 4] = term if sums[m % 4] is None else sums[m % 4] + term
        out_buf[rows, :] = q_ref[rows, :] * ((sums[0] + sums[1]) + (sums[2] + sums[3]))
    y_ref[...] = out_buf[...].astype(bf16)


def close(place, z_two, q_li, seg, part, totals, poles, residues, skip_li, near_count):
    tok_rows, channels = z_two.shape
    modes = poles.shape[0]
    column = lambda rows: pl.BlockSpec((rows, LANES), lambda i: (0, i))
    return pl.pallas_call(
        lambda *refs: close_kernel(near_count, *refs),
        grid=(channels // LANES,),
        in_specs=[
            pl.BlockSpec(memory_space=pltpu.SMEM),
            column(tok_rows),
            column(tok_rows),
            column(modes * SEGMENTS),
            column(modes),
            pl.BlockSpec((totals.shape[0], modes, LANES), lambda i: (0, 0, i)),
            column(modes),
            column(modes),
            column(1),
        ],
        out_specs=column(tok_rows),
        out_shape=jax.ShapeDtypeStruct((tok_rows, channels), bf16),
        scratch_shapes=[
            pltpu.VMEM((modes * SEGMENTS, LANES), f32),
            pltpu.VMEM((tok_rows, LANES), f32),
        ],
        compiler_params=small(60.15),
        name="close",
    )(place, z_two, q_li, seg, part, totals, poles, residues, skip_li.reshape(1, channels))


def project_kernel(order, core_first, place_ref, y_ref, w_ref, *refs):
    if core_first:
        (out_ref, w_buf, sems) = refs
    else:
        (half_ref, residual_ref, out_ref, w_buf, sems) = refs
    count = y_ref.shape[0]
    copies = [
        pltpu.make_async_copy(w_ref.at[(place_ref[0] + order[k]) % count, place_ref[1]], w_buf.at[k], sems.at[k])
        for k in range(count)
    ]
    for copy in copies:
        copy.start()
    total = None
    for k in range(count):
        copies[k].wait()
        term = jnp.dot(y_ref[k], w_buf[k], preferred_element_type=f32)
        total = term if total is None else total + term
    if core_first:
        out_ref[...] = total
    else:
        out_ref[...] = (residual_ref[...].astype(f32) + (half_ref[...] + total)).astype(bf16)


def project(order, place, pieces, w_all, extra):
    count, tok_rows, depth = pieces.shape
    columns = w_all.shape[1]
    vmem = pl.BlockSpec(memory_space=pltpu.VMEM)
    return pl.pallas_call(
        lambda *refs: project_kernel(order, not extra, *refs),
        in_specs=[pl.BlockSpec(memory_space=pltpu.SMEM), vmem, pl.BlockSpec(memory_space=pltpu.HBM)]
        + [vmem] * len(extra),
        out_specs=vmem,
        out_shape=jax.ShapeDtypeStruct((tok_rows, columns), bf16 if extra else f32),
        scratch_shapes=[
            pltpu.VMEM((count, depth, columns), bf16),
            pltpu.SemaphoreType.DMA((count,)),
        ],
        cost_estimate=pl.CostEstimate(
            flops=2 * count * tok_rows * depth * columns,
            bytes_accessed=2 * count * depth * (tok_rows + columns),
            transcendentals=0,
        ),
        compiler_params=small(54),
        name="second_half" if extra else "first_half",
    )(place, pieces, w_all.reshape(count, 2, depth, columns), *extra)


def tail_kernel(feat_ref, gate_ref, out_ref, sems):
    tok_rows = feat_ref.shape[1]
    at, copies = 0, []
    for ref, stream, rows in (
        (feat_ref, 1, FRONT),
        (feat_ref, 2, FRONT),
        (feat_ref, 0, REACH),
        (gate_ref, 0, REACH),
        (gate_ref, 1, REACH),
    ):
        source = ref.at[stream, pl.ds(tok_rows - rows, rows)]
        copies.append(pltpu.make_async_copy(source, out_ref.at[pl.ds(at, rows)], sems.at[len(copies)]))
        at += rows
    for copy in copies:
        copy.start()
    for copy in copies:
        copy.wait()


def tails(features, gates):
    return pl.pallas_call(
        tail_kernel,
        in_specs=[pl.BlockSpec(memory_space=pltpu.HBM)] * 2,
        out_specs=pl.BlockSpec(memory_space=pltpu.VMEM),
        out_shape=pltpu.VMEM((2 * FRONT + 3 * REACH, features.shape[2]), bf16),
        scratch_shapes=[pltpu.SemaphoreType.DMA((5,))],
        compiler_params=small(60.15),
        name="tails",
    )(features, gates)


NEAR = 4


def on_device(
    residual_in, features, short_mr, medium, skip_mr, li_gates, short_li, poles, residues, skip_li, w_out,
):
    seq_count, tp_count = lax.axis_size("seq"), lax.axis_size("tp")
    rows_count = seq_count // NEAR
    tok_rows = features.shape[1]
    seq_at, tp_at = lax.axis_index("seq"), lax.axis_index("tp")
    place = jnp.stack([seq_at // NEAR, seq_at % NEAR]).astype(jnp.int32)

    w_all = lax.all_gather(w_out, "seq", axis=0, tiled=True)

    tail = tails(features, li_gates)
    halo = lax.ppermute(tail, "seq", [(i, i + 1) for i in range(seq_count - 1)])
    bands = make_bands(medium)
    z_two, q_li, seg, ends = mix(
        features, li_gates, halo, short_mr, short_li, skip_mr, bands, poles, NEAR
    )
    near_groups = [[row * NEAR + i for i in range(NEAR)] for row in range(rows_count)]
    far_groups = [[row * NEAR + i for row in range(rows_count)] for i in range(NEAR)]
    ends = lax.all_to_all(ends, "seq", 0, 0, tiled=True, axis_index_groups=near_groups)
    part, total = near(place, ends, poles, tok_rows, rows_count)
    totals = lax.all_to_all(total, "seq", 0, 0, tiled=True, axis_index_groups=far_groups)
    y_two = close(place, z_two, q_li, seg, part, totals, poles, residues, skip_li, NEAR)

    chips = tp_count // 2
    order = sorted(range(chips), key=lambda k: -min(k, chips - k))
    own = jnp.stack(
        [
            lax.ppermute(y_two, "tp", [((t + 2 * k) % tp_count, t) for t in range(tp_count)]) if k else y_two
            for k in order
        ]
    )
    other = lax.ppermute(own, "tp", [(t, t ^ 1) for t in range(tp_count)])
    chip_at, core_at = tp_at // 2, tp_at % 2
    here = jnp.stack([chip_at, core_at]).astype(jnp.int32)
    there = jnp.stack([chip_at, 1 - core_at]).astype(jnp.int32)
    half = project(order, here, own, w_all, ())
    return project(order, there, other, w_all, (half, residual_in))


def solution(mesh):
    placed = (
        P("seq", "tp"),
        P(None, "seq", "tp"),
        P(None, None, "tp"),
        P(None, "tp"),
        P("tp"),
        P(None, "seq", "tp"),
        P(None, None, "tp"),
        P(None, "tp"),
        P(None, "tp"),
        P("tp"),
        P("seq", "tp"),
    )
    return jax.shard_map(
        on_device, mesh=mesh, in_specs=placed, out_specs=P("seq", "tp"), check_vma=False
    )
```

```python
import jax
import jax.numpy as jnp
from jax import lax
from jax.experimental import pallas as pl
from jax.experimental.pallas import tpu as pltpu
from jax.sharding import PartitionSpec as P

f32 = jnp.float32
bf16 = jnp.bfloat16
LANES = 128
SEGMENTS = 8
FRONT = 144
REACH = 16


def small(mebibytes):
    return pltpu.CompilerParams(vmem_limit_bytes=int(mebibytes * 1024) * 1024)


def power(base, exponent):
    result, square = None, base
    while exponent:
        if exponent & 1:
            result = square if result is None else result * square
        exponent >>= 1
        if exponent:
            square = square * square
    return result


def bands_kernel(line_ref, out_ref):
    for group in range(out_ref.shape[0]):
        rows = jnp.broadcast_to(line_ref[group : group + 1, :], out_ref.shape[1:])
        out_ref[group] = pltpu.roll(rows, 0, 1, stride=1, stride_axis=0).astype(bf16)


def make_bands(medium):
    taps, groups = medium.shape
    line = jnp.concatenate(
        [jnp.zeros((1, groups), medium.dtype), medium[::-1], jnp.zeros((taps - 1, groups), medium.dtype)]
    )
    per_step = 8
    return pl.pallas_call(
        bands_kernel,
        grid=(groups // per_step,),
        in_specs=[pl.BlockSpec((per_step, 2 * taps), lambda i: (i, 0))],
        out_specs=pl.BlockSpec((per_step, taps, 2 * taps), lambda i: (i, 0, 0)),
        out_shape=jax.ShapeDtypeStruct((groups, taps, 2 * taps), bf16),
        compiler_params=small(8),
        name="bands",
    )(line.T.astype(f32))


def conv_rows(buffer, taps, first, count):
    total = None
    for lag in range(len(taps)):
        term = taps[lag] * buffer[pl.ds(first - lag, count), :]
        total = term if total is None else total + term
    return total


def mix_kernel(
    feat_ref, gate_ref, halo_ref, short_mr_ref, short_li_ref, skip_ref, band_ref, pole_ref,
    z_ref, q_ref, seg_ref, end_ref,
    k_buf, v_buf, s_buf, y_buf, zwin, state_buf, med_buf,
):
    tok_rows = feat_ref.shape[1]
    taps_med = band_ref.shape[1]
    groups = band_ref.shape[0]
    group_width = LANES // groups
    n_short = short_mr_ref.shape[1]
    step = 32

    def taps_of(ref, stream):
        return [ref[stream, lag : lag + 1, :] for lag in range(n_short)]

    for buf, at, stream in ((k_buf, 0, 1), (v_buf, FRONT, 2)):
        buf[0:8, :] = jnp.zeros((8, LANES), f32)
        buf[8 : 8 + FRONT, :] = halo_ref[at : at + FRONT, :].astype(f32)
        buf[8 + FRONT :, :] = feat_ref[stream].astype(f32)
    k_taps, v_taps = taps_of(short_mr_ref, 1), taps_of(short_mr_ref, 2)
    lead = 2 * taps_med - FRONT
    zwin[0:lead, :] = jnp.zeros((lead, LANES), bf16)
    for first in range(0, FRONT + tok_rows, 16):
        count = 16
        k_part = conv_rows(k_buf, k_taps, 8 + first, count)
        v_part = conv_rows(v_buf, v_taps, 8 + first, count)
        zwin[lead + first : lead + first + count, :] = (k_part * v_part).astype(bf16)

    owner = lax.broadcasted_iota(jnp.int32, (8, LANES), 1) // group_width
    masks = [owner == group for group in range(groups)]

    def pick(product, rows, start):
        for r in range(0, rows, 8):
            total = product[r : r + 8]
            for group in range(1, groups):
                total = jnp.where(masks[group], product[group * rows + r : group * rows + r + 8], total)
            med_buf[start + r : start + r + 8, :] = total

    tail = band_ref[:, taps_med - 16 :, :].reshape(groups * 16, 2 * taps_med)
    pick(jnp.dot(tail, zwin[0 : 2 * taps_med, :], preferred_element_type=f32), 16, 0)
    whole = band_ref[...].reshape(groups * taps_med, 2 * taps_med)
    for block in range(tok_rows // taps_med):
        window = zwin[taps_med * (block + 1) : taps_med * (block + 3), :]
        pick(jnp.dot(whole, window, preferred_element_type=f32), taps_med, 16 + taps_med * block)

    s_buf[0:16, :] = halo_ref[2 * FRONT : 2 * FRONT + 16, :].astype(f32)
    s_buf[16:, :] = feat_ref[0].astype(f32)
    q_taps = taps_of(short_mr_ref, 0)
    skip = skip_ref[...]
    z_last = 2 * taps_med
    q_part = conv_rows(s_buf, q_taps, 8, 8)
    z_part = zwin[z_last - 16 : z_last, :].astype(f32)[8:16]
    y_buf[0:8, :] = (q_part * (med_buf[8:16, :] + skip * z_part)).astype(bf16).astype(f32)
    for first in range(0, tok_rows, step):
        q_part = conv_rows(s_buf, q_taps, 16 + first, step)
        z_part = zwin[z_last + first : z_last + first + step, :].astype(f32)
        y_part = q_part * (med_buf[16 + first : 16 + first + step, :] + skip * z_part)
        y_buf[8 + first : 8 + first + step, :] = y_part.astype(bf16).astype(f32)

    for buf, at, stream in ((k_buf, 16, 0), (v_buf, 32, 1)):
        tail_rows = halo_ref[2 * FRONT + at : 2 * FRONT + at + 16, :].astype(f32)
        buf[0:8, :] = tail_rows[8:16]
        buf[8 : 8 + tok_rows, :] = gate_ref[stream].astype(f32)
    li_taps = [taps_of(short_li_ref, i) for i in range(3)]
    for first in range(0, tok_rows, step):
        rows = slice(first, first + step)
        q_ref[rows, :] = conv_rows(k_buf, li_taps[0], 8 + first, step)
        k_part = conv_rows(v_buf, li_taps[1], 8 + first, step)
        z_ref[rows, :] = k_part * conv_rows(y_buf, li_taps[2], 8 + first, step)

    modes = pole_ref.shape[0]
    seg_rows = tok_rows // SEGMENTS
    pole = [jnp.broadcast_to(pole_ref[m : m + 1, :], (SEGMENTS, LANES)) for m in range(modes)]
    state = [None] * modes
    for t in range(seg_rows):
        z_now = z_ref[pl.ds(t, SEGMENTS, stride=seg_rows), :]
        state = [z_now if s is None else pole[m] * s + z_now for m, s in enumerate(state)]
    for m in range(modes):
        state_buf[m * SEGMENTS : (m + 1) * SEGMENTS, :] = state[m]
    seg_decay = power(pole_ref[...], seg_rows)
    total = state_buf[pl.ds(0, modes, stride=SEGMENTS), :]
    for s in range(1, SEGMENTS):
        total = seg_decay * total + state_buf[pl.ds(s, modes, stride=SEGMENTS), :]
    seg_ref[...] = state_buf[...]
    for copy in range(end_ref.shape[0]):
        end_ref[copy] = total


def mix(features, gates, halo, short_mr, short_li, skip_mr, bands, poles, copies):
    tok_rows, channels = features.shape[1:]
    modes = poles.shape[0]
    groups = bands.shape[0]
    tiles = channels // LANES
    per_tile = groups // tiles
    taps_med = bands.shape[1]
    shapes = [
        ((tok_rows, channels), (tok_rows, LANES), lambda i: (0, i)),
        ((tok_rows, channels), (tok_rows, LANES), lambda i: (0, i)),
        ((modes * SEGMENTS, channels), (modes * SEGMENTS, LANES), lambda i: (0, i)),
        ((copies, modes, channels), (copies, modes, LANES), lambda i: (0, 0, i)),
    ]
    return pl.pallas_call(
        mix_kernel,
        grid=(tiles,),
        in_specs=[
            pl.BlockSpec((3, tok_rows, LANES), lambda i: (0, 0, i)),
            pl.BlockSpec((2, tok_rows, LANES), lambda i: (0, 0, i)),
            pl.BlockSpec((halo.shape[0], LANES), lambda i: (0, i)),
            pl.BlockSpec((3, short_mr.shape[1], LANES), lambda i: (0, 0, i)),
            pl.BlockSpec((3, short_li.shape[1], LANES), lambda i: (0, 0, i)),
            pl.BlockSpec((1, LANES), lambda i: (0, i)),
            pl.BlockSpec((per_tile, taps_med, 2 * taps_med), lambda i: (i, 0, 0)),
            pl.BlockSpec((modes, LANES), lambda i: (0, i)),
        ],
        out_specs=[pl.BlockSpec(block, index) for _, block, index in shapes],
        out_shape=[pltpu.HBM(shape, f32) for shape, _, _ in shapes],
        scratch_shapes=[
            pltpu.VMEM((8 + FRONT + tok_rows, LANES), f32),
            pltpu.VMEM((8 + FRONT + tok_rows, LANES), f32),
            pltpu.VMEM((16 + tok_rows, LANES), f32),
            pltpu.VMEM((8 + tok_rows, LANES), f32),
            pltpu.VMEM((2 * taps_med + tok_rows, LANES), bf16),
            pltpu.VMEM((modes * SEGMENTS, LANES), f32),
            pltpu.VMEM((16 + tok_rows, LANES), f32),
        ],
        compiler_params=small(16),
        name="mix",
    )(features, gates, halo, short_mr, short_li, skip_mr.reshape(1, channels), bands, poles)


def near_kernel(tok_rows, place_ref, ends_ref, pole_ref, part_ref, total_ref):
    mine = place_ref[1]
    decay = power(pole_ref[...], tok_rows)
    part = jnp.zeros(decay.shape, f32)
    total = jnp.zeros(decay.shape, f32)
    for other in range(ends_ref.shape[0]):
        end = ends_ref[other]
        part = jnp.where(other < mine, decay * part + end, part)
        total = decay * total + end
    part_ref[...] = part
    for copy in range(total_ref.shape[0]):
        total_ref[copy] = total


def near(place, ends, poles, tok_rows, copies):
    return pl.pallas_call(
        lambda *refs: near_kernel(tok_rows, *refs),
        in_specs=[
            pl.BlockSpec(memory_space=pltpu.SMEM),
            pl.BlockSpec(memory_space=pltpu.VMEM),
            pl.BlockSpec(memory_space=pltpu.VMEM),
        ],
        out_shape=[
            jax.ShapeDtypeStruct(poles.shape, f32),
            jax.ShapeDtypeStruct((copies, *poles.shape), f32),
        ],
        compiler_params=small(4),
        name="near",
    )(place, ends, poles)


def close_kernel(
    near_count, place_ref, z_ref, q_ref, seg_ref, part_ref, total_ref, pole_ref, res_ref, skip_ref,
    y_ref, state_buf, out_buf,
):
    tok_rows = z_ref.shape[0]
    modes = pole_ref.shape[0]
    seg_rows = tok_rows // SEGMENTS
    row, mine = place_ref[0], place_ref[1]
    seg_decay = power(pole_ref[...], seg_rows)
    decay = power(seg_decay, SEGMENTS)
    row_decay = power(decay, near_count)
    far = jnp.zeros(decay.shape, f32)
    for other in range(total_ref.shape[0]):
        far = jnp.where(other < row, row_decay * far + total_ref[other], far)
    for step in range(near_count - 1):
        far = jnp.where(step < mine, decay * far, far)
    start = far + part_ref[...]
    for s in range(SEGMENTS):
        state_buf[pl.ds(s, modes, stride=SEGMENTS), :] = start
        if s < SEGMENTS - 1:
            start = seg_decay * start + seg_ref[pl.ds(s, modes, stride=SEGMENTS), :]
    state = [state_buf[m * SEGMENTS : (m + 1) * SEGMENTS, :] for m in range(modes)]
    pole = [jnp.broadcast_to(pole_ref[m : m + 1, :], (SEGMENTS, LANES)) for m in range(modes)]
    gain = [jnp.broadcast_to(res_ref[m : m + 1, :], (SEGMENTS, LANES)) for m in range(modes)]
    skip = jnp.broadcast_to(skip_ref[...], (SEGMENTS, LANES))
    for t in range(seg_rows):
        rows = pl.ds(t, SEGMENTS, stride=seg_rows)
        z_now = z_ref[rows, :]
        sums = [skip * z_now, None, None, None]
        for m in range(modes):
            state[m] = pole[m] * state[m] + z_now
            term = gain[m] * state[m]
            sums[m % 4] = term if sums[m % 4] is None else sums[m % 4] + term
        out_buf[rows, :] = q_ref[rows, :] * ((sums[0] + sums[1]) + (sums[2] + sums[3]))
    y_ref[...] = out_buf[...].astype(bf16)


def close(place, z_two, q_li, seg, part, totals, poles, residues, skip_li, near_count):
    tok_rows, channels = z_two.shape
    modes = poles.shape[0]
    column = lambda rows: pl.BlockSpec((rows, LANES), lambda i: (0, i))
    return pl.pallas_call(
        lambda *refs: close_kernel(near_count, *refs),
        grid=(channels // LANES,),
        in_specs=[
            pl.BlockSpec(memory_space=pltpu.SMEM),
            column(tok_rows),
            column(tok_rows),
            column(modes * SEGMENTS),
            column(modes),
            pl.BlockSpec((totals.shape[0], modes, LANES), lambda i: (0, 0, i)),
            column(modes),
            column(modes),
            column(1),
        ],
        out_specs=column(tok_rows),
        out_shape=jax.ShapeDtypeStruct((tok_rows, channels), bf16),
        scratch_shapes=[
            pltpu.VMEM((modes * SEGMENTS, LANES), f32),
            pltpu.VMEM((tok_rows, LANES), f32),
        ],
        compiler_params=small(60.15),
        name="close",
    )(place, z_two, q_li, seg, part, totals, poles, residues, skip_li.reshape(1, channels))


def project_kernel(place_ref, own_ref, other_ref, w_ref, residual_ref, out_ref, w_buf, w_sems):
    count = own_ref.shape[0]
    copies = []
    for half in range(2):
        core = place_ref[1] if half == 0 else 1 - place_ref[1]
        for k in range(count):
            chip = (place_ref[0] + ORDER[k] + count) % count
            i = half * count + k
            copies.append(pltpu.make_async_copy(w_ref.at[chip, core], w_buf.at[i], w_sems.at[i]))
    for copy in copies:
        copy.start()
    total = residual_ref[...].astype(f32)
    for i, copy in enumerate(copies):
        y_ref = own_ref if i < count else other_ref
        copy.wait()
        total += jnp.dot(y_ref[i % count], w_buf[i], preferred_element_type=f32)
    out_ref[...] = total.astype(bf16)


def project(place, own, other, w_all, residual):
    count, tok_rows, depth = own.shape
    columns = w_all.shape[1]
    vmem = pl.BlockSpec(memory_space=pltpu.VMEM)
    w_all = pltpu.with_memory_space_constraint(w_all.reshape(count, 2, depth, columns), pltpu.HBM)
    return pl.pallas_call(
        project_kernel,
        in_specs=[pl.BlockSpec(memory_space=pltpu.SMEM), vmem, vmem, pl.BlockSpec(memory_space=pltpu.HBM), vmem],
        out_specs=vmem,
        out_shape=jax.ShapeDtypeStruct((tok_rows, columns), bf16),
        scratch_shapes=[
            pltpu.VMEM((2 * count, depth, columns), bf16),
            pltpu.SemaphoreType.DMA((2 * count,)),
        ],
        cost_estimate=pl.CostEstimate(
            flops=4 * count * tok_rows * depth * columns,
            bytes_accessed=4 * count * depth * (tok_rows + columns),
            transcendentals=0,
        ),
        compiler_params=small(20),
        name="project",
    )(place, own, other, w_all, residual)


def tail_kernel(feat_ref, gate_ref, out_ref, sems):
    tok_rows = feat_ref.shape[1]
    at, copies = 0, []
    for ref, stream, rows in (
        (feat_ref, 1, FRONT),
        (feat_ref, 2, FRONT),
        (feat_ref, 0, REACH),
        (gate_ref, 0, REACH),
        (gate_ref, 1, REACH),
    ):
        source = ref.at[stream, pl.ds(tok_rows - rows, rows)]
        copies.append(pltpu.make_async_copy(source, out_ref.at[pl.ds(at, rows)], sems.at[len(copies)]))
        at += rows
    for copy in copies:
        copy.start()
    for copy in copies:
        copy.wait()


def tails(features, gates):
    return pl.pallas_call(
        tail_kernel,
        in_specs=[pl.BlockSpec(memory_space=pltpu.HBM)] * 2,
        out_specs=pl.BlockSpec(memory_space=pltpu.VMEM),
        out_shape=pltpu.VMEM((2 * FRONT + 3 * REACH, features.shape[2]), bf16),
        scratch_shapes=[pltpu.SemaphoreType.DMA((5,))],
        compiler_params=small(60.15),
        name="tails",
    )(features, gates)


ORDER = (0, 1, -1, 2, -2, 3, -3, 4)
NEAR = 4


def on_device(
    residual_in, features, short_mr, medium, skip_mr, li_gates, short_li, poles, residues, skip_li, w_out,
):
    seq_count, tp_count = lax.axis_size("seq"), lax.axis_size("tp")
    rows_count = seq_count // NEAR
    tok_rows = features.shape[1]
    seq_at, tp_at = lax.axis_index("seq"), lax.axis_index("tp")
    place = jnp.stack([seq_at // NEAR, seq_at % NEAR]).astype(jnp.int32)

    w_all = lax.all_gather(w_out, "seq", axis=0, tiled=True)

    tail = tails(features, li_gates)
    halo = lax.ppermute(tail, "seq", [(i, i + 1) for i in range(seq_count - 1)])
    bands = make_bands(medium)
    z_two, q_li, seg, ends = mix(
        features, li_gates, halo, short_mr, short_li, skip_mr, bands, poles, NEAR
    )
    near_groups = [[row * NEAR + i for i in range(NEAR)] for row in range(rows_count)]
    far_groups = [[row * NEAR + i for row in range(rows_count)] for i in range(NEAR)]
    ends = lax.all_to_all(ends, "seq", 0, 0, tiled=True, axis_index_groups=near_groups)
    part, total = near(place, ends, poles, tok_rows, rows_count)
    totals = lax.all_to_all(total, "seq", 0, 0, tiled=True, axis_index_groups=far_groups)
    y_two = close(place, z_two, q_li, seg, part, totals, poles, residues, skip_li, NEAR)

    up = [((t + 2) % tp_count, t) for t in range(tp_count)]
    down = [((t - 2) % tp_count, t) for t in range(tp_count)]
    ahead, behind = y_two, y_two
    pieces = {0: y_two}
    for step in range(1, tp_count // 4 + 1):
        ahead = lax.ppermute(ahead, "tp", up)
        pieces[step] = ahead
        if step < tp_count // 4:
            behind = lax.ppermute(behind, "tp", down)
            pieces[-step] = behind
    own = jnp.stack([pieces[k] for k in ORDER])
    other = lax.ppermute(own, "tp", [(t, t ^ 1) for t in range(tp_count)])
    other = pltpu.with_memory_space_constraint(other, pltpu.VMEM)
    here = jnp.stack([tp_at // 2, tp_at % 2]).astype(jnp.int32)
    return project(here, own, other, w_all, residual_in)


def solution(mesh):
    placed = (
        P("seq", "tp"),
        P(None, "seq", "tp"),
        P(None, None, "tp"),
        P(None, "tp"),
        P("tp"),
        P(None, "seq", "tp"),
        P(None, None, "tp"),
        P(None, "tp"),
        P(None, "tp"),
        P("tp"),
        P("seq", "tp"),
    )
    return jax.shard_map(
        on_device, mesh=mesh, in_specs=placed, out_specs=P("seq", "tp"), check_vma=False
    )
```

```python
import jax
import jax.numpy as jnp
from jax import lax
from jax.experimental import pallas as pl
from jax.experimental.pallas import tpu as pltpu
from jax.sharding import PartitionSpec as P

f32 = jnp.float32
bf16 = jnp.bfloat16
LANES = 128
SEGMENTS = 8
FRONT = 144
REACH = 16


def small(mebibytes):
    return pltpu.CompilerParams(vmem_limit_bytes=int(mebibytes * 1024) * 1024)


def power(base, exponent):
    result, square = None, base
    while exponent:
        if exponent & 1:
            result = square if result is None else result * square
        exponent >>= 1
        if exponent:
            square = square * square
    return result


def bands_kernel(line_ref, out_ref):
    for group in range(out_ref.shape[0]):
        rows = jnp.broadcast_to(line_ref[group : group + 1, :], out_ref.shape[1:])
        out_ref[group] = pltpu.roll(rows, 0, 1, stride=1, stride_axis=0).astype(bf16)


def make_bands(medium):
    taps, groups = medium.shape
    line = jnp.concatenate(
        [jnp.zeros((1, groups), medium.dtype), medium[::-1], jnp.zeros((taps - 1, groups), medium.dtype)]
    )
    per_step = 8
    return pl.pallas_call(
        bands_kernel,
        grid=(groups // per_step,),
        in_specs=[pl.BlockSpec((per_step, 2 * taps), lambda i: (i, 0))],
        out_specs=pl.BlockSpec((per_step, taps, 2 * taps), lambda i: (i, 0, 0)),
        out_shape=jax.ShapeDtypeStruct((groups, taps, 2 * taps), bf16),
        compiler_params=small(8),
        name="bands",
    )(line.T.astype(f32))


def conv_rows(buffer, taps, first, count):
    total = None
    for lag in range(len(taps)):
        term = taps[lag] * buffer[pl.ds(first - lag, count), :]
        total = term if total is None else total + term
    return total


def mix_kernel(
    feat_ref, gate_ref, halo_ref, short_mr_ref, short_li_ref, skip_ref, band_ref, pole_ref,
    z_ref, q_ref, seg_ref, end_ref,
    k_buf, v_buf, s_buf, y_buf, zwin, state_buf, med_buf,
):
    tok_rows = feat_ref.shape[1]
    taps_med = band_ref.shape[1]
    groups = band_ref.shape[0]
    group_width = LANES // groups
    n_short = short_mr_ref.shape[1]
    step = 32

    def taps_of(ref, stream):
        return [ref[stream, lag : lag + 1, :] for lag in range(n_short)]

    for buf, at, stream in ((k_buf, 0, 1), (v_buf, FRONT, 2)):
        buf[0:8, :] = jnp.zeros((8, LANES), f32)
        buf[8 : 8 + FRONT, :] = halo_ref[at : at + FRONT, :].astype(f32)
        buf[8 + FRONT :, :] = feat_ref[stream].astype(f32)
    k_taps, v_taps = taps_of(short_mr_ref, 1), taps_of(short_mr_ref, 2)
    lead = 2 * taps_med - FRONT
    zwin[0:lead, :] = jnp.zeros((lead, LANES), bf16)
    for first in range(0, FRONT + tok_rows, 16):
        count = 16
        k_part = conv_rows(k_buf, k_taps, 8 + first, count)
        v_part = conv_rows(v_buf, v_taps, 8 + first, count)
        zwin[lead + first : lead + first + count, :] = (k_part * v_part).astype(bf16)

    owner = lax.broadcasted_iota(jnp.int32, (8, LANES), 1) // group_width
    masks = [owner == group for group in range(groups)]

    def pick(product, rows, start):
        for r in range(0, rows, 8):
            total = product[r : r + 8]
            for group in range(1, groups):
                total = jnp.where(masks[group], product[group * rows + r : group * rows + r + 8], total)
            med_buf[start + r : start + r + 8, :] = total

    tail = band_ref[:, taps_med - 16 :, :].reshape(groups * 16, 2 * taps_med)
    pick(jnp.dot(tail, zwin[0 : 2 * taps_med, :], preferred_element_type=f32), 16, 0)
    whole = band_ref[...].reshape(groups * taps_med, 2 * taps_med)
    for block in range(tok_rows // taps_med):
        window = zwin[taps_med * (block + 1) : taps_med * (block + 3), :]
        pick(jnp.dot(whole, window, preferred_element_type=f32), taps_med, 16 + taps_med * block)

    s_buf[0:16, :] = halo_ref[2 * FRONT : 2 * FRONT + 16, :].astype(f32)
    s_buf[16:, :] = feat_ref[0].astype(f32)
    q_taps = taps_of(short_mr_ref, 0)
    skip = skip_ref[...]
    z_last = 2 * taps_med
    q_part = conv_rows(s_buf, q_taps, 8, 8)
    z_part = zwin[z_last - 16 : z_last, :].astype(f32)[8:16]
    y_buf[0:8, :] = (q_part * (med_buf[8:16, :] + skip * z_part)).astype(bf16).astype(f32)
    for first in range(0, tok_rows, step):
        q_part = conv_rows(s_buf, q_taps, 16 + first, step)
        z_part = zwin[z_last + first : z_last + first + step, :].astype(f32)
        y_part = q_part * (med_buf[16 + first : 16 + first + step, :] + skip * z_part)
        y_buf[8 + first : 8 + first + step, :] = y_part.astype(bf16).astype(f32)

    for buf, at, stream in ((k_buf, 16, 0), (v_buf, 32, 1)):
        tail_rows = halo_ref[2 * FRONT + at : 2 * FRONT + at + 16, :].astype(f32)
        buf[0:8, :] = tail_rows[8:16]
        buf[8 : 8 + tok_rows, :] = gate_ref[stream].astype(f32)
    li_taps = [taps_of(short_li_ref, i) for i in range(3)]
    for first in range(0, tok_rows, step):
        rows = slice(first, first + step)
        q_ref[rows, :] = conv_rows(k_buf, li_taps[0], 8 + first, step)
        k_part = conv_rows(v_buf, li_taps[1], 8 + first, step)
        z_ref[rows, :] = k_part * conv_rows(y_buf, li_taps[2], 8 + first, step)

    modes = pole_ref.shape[0]
    seg_rows = tok_rows // SEGMENTS
    pole = [jnp.broadcast_to(pole_ref[m : m + 1, :], (SEGMENTS, LANES)) for m in range(modes)]
    state = [None] * modes
    for t in range(seg_rows):
        z_now = z_ref[pl.ds(t, SEGMENTS, stride=seg_rows), :]
        state = [z_now if s is None else pole[m] * s + z_now for m, s in enumerate(state)]
    for m in range(modes):
        state_buf[m * SEGMENTS : (m + 1) * SEGMENTS, :] = state[m]
    seg_decay = power(pole_ref[...], seg_rows)
    total = state_buf[pl.ds(0, modes, stride=SEGMENTS), :]
    for s in range(1, SEGMENTS):
        total = seg_decay * total + state_buf[pl.ds(s, modes, stride=SEGMENTS), :]
    seg_ref[...] = state_buf[...]
    for copy in range(end_ref.shape[0]):
        end_ref[copy] = total


def mix(features, gates, halo, short_mr, short_li, skip_mr, bands, poles, copies):
    tok_rows, channels = features.shape[1:]
    modes = poles.shape[0]
    groups = bands.shape[0]
    tiles = channels // LANES
    per_tile = groups // tiles
    taps_med = bands.shape[1]
    shapes = [
        ((tok_rows, channels), (tok_rows, LANES), lambda i: (0, i)),
        ((tok_rows, channels), (tok_rows, LANES), lambda i: (0, i)),
        ((modes * SEGMENTS, channels), (modes * SEGMENTS, LANES), lambda i: (0, i)),
        ((copies, modes, channels), (copies, modes, LANES), lambda i: (0, 0, i)),
    ]
    return pl.pallas_call(
        mix_kernel,
        grid=(tiles,),
        in_specs=[
            pl.BlockSpec((3, tok_rows, LANES), lambda i: (0, 0, i)),
            pl.BlockSpec((2, tok_rows, LANES), lambda i: (0, 0, i)),
            pl.BlockSpec((halo.shape[0], LANES), lambda i: (0, i)),
            pl.BlockSpec((3, short_mr.shape[1], LANES), lambda i: (0, 0, i)),
            pl.BlockSpec((3, short_li.shape[1], LANES), lambda i: (0, 0, i)),
            pl.BlockSpec((1, LANES), lambda i: (0, i)),
            pl.BlockSpec((per_tile, taps_med, 2 * taps_med), lambda i: (i, 0, 0)),
            pl.BlockSpec((modes, LANES), lambda i: (0, i)),
        ],
        out_specs=[pl.BlockSpec(block, index) for _, block, index in shapes],
        out_shape=[pltpu.HBM(shape, f32) for shape, _, _ in shapes],
        scratch_shapes=[
            pltpu.VMEM((8 + FRONT + tok_rows, LANES), f32),
            pltpu.VMEM((8 + FRONT + tok_rows, LANES), f32),
            pltpu.VMEM((16 + tok_rows, LANES), f32),
            pltpu.VMEM((8 + tok_rows, LANES), f32),
            pltpu.VMEM((2 * taps_med + tok_rows, LANES), bf16),
            pltpu.VMEM((modes * SEGMENTS, LANES), f32),
            pltpu.VMEM((16 + tok_rows, LANES), f32),
        ],
        compiler_params=small(16),
        name="mix",
    )(features, gates, halo, short_mr, short_li, skip_mr.reshape(1, channels), bands, poles)


def near_kernel(tok_rows, place_ref, ends_ref, pole_ref, part_ref, total_ref):
    mine = place_ref[1]
    decay = power(pole_ref[...], tok_rows)
    part = jnp.zeros(decay.shape, f32)
    total = jnp.zeros(decay.shape, f32)
    for other in range(ends_ref.shape[0]):
        end = ends_ref[other]
        part = jnp.where(other < mine, decay * part + end, part)
        total = decay * total + end
    part_ref[...] = part
    for copy in range(total_ref.shape[0]):
        total_ref[copy] = total


def near(place, ends, poles, tok_rows, copies):
    return pl.pallas_call(
        lambda *refs: near_kernel(tok_rows, *refs),
        in_specs=[
            pl.BlockSpec(memory_space=pltpu.SMEM),
            pl.BlockSpec(memory_space=pltpu.VMEM),
            pl.BlockSpec(memory_space=pltpu.VMEM),
        ],
        out_shape=[
            jax.ShapeDtypeStruct(poles.shape, f32),
            jax.ShapeDtypeStruct((copies, *poles.shape), f32),
        ],
        compiler_params=small(4),
        name="near",
    )(place, ends, poles)


def close_kernel(
    near_count, place_ref, z_ref, q_ref, seg_ref, part_ref, total_ref, pole_ref, res_ref, skip_ref,
    y_ref, state_buf, out_buf,
):
    tok_rows = z_ref.shape[0]
    modes = pole_ref.shape[0]
    seg_rows = tok_rows // SEGMENTS
    row, mine = place_ref[0], place_ref[1]
    seg_decay = power(pole_ref[...], seg_rows)
    decay = power(seg_decay, SEGMENTS)
    row_decay = power(decay, near_count)
    far = jnp.zeros(decay.shape, f32)
    for other in range(total_ref.shape[0]):
        far = jnp.where(other < row, row_decay * far + total_ref[other], far)
    for step in range(near_count - 1):
        far = jnp.where(step < mine, decay * far, far)
    start = far + part_ref[...]
    for s in range(SEGMENTS):
        state_buf[pl.ds(s, modes, stride=SEGMENTS), :] = start
        if s < SEGMENTS - 1:
            start = seg_decay * start + seg_ref[pl.ds(s, modes, stride=SEGMENTS), :]
    state = [state_buf[m * SEGMENTS : (m + 1) * SEGMENTS, :] for m in range(modes)]
    pole = [jnp.broadcast_to(pole_ref[m : m + 1, :], (SEGMENTS, LANES)) for m in range(modes)]
    gain = [jnp.broadcast_to(res_ref[m : m + 1, :], (SEGMENTS, LANES)) for m in range(modes)]
    skip = jnp.broadcast_to(skip_ref[...], (SEGMENTS, LANES))
    for t in range(seg_rows):
        rows = pl.ds(t, SEGMENTS, stride=seg_rows)
        z_now = z_ref[rows, :]
        sums = [skip * z_now, None, None, None]
        for m in range(modes):
            state[m] = pole[m] * state[m] + z_now
            term = gain[m] * state[m]
            sums[m % 4] = term if sums[m % 4] is None else sums[m % 4] + term
        out_buf[rows, :] = q_ref[rows, :] * ((sums[0] + sums[1]) + (sums[2] + sums[3]))
    y_ref[...] = out_buf[...].astype(bf16)


def close(place, z_two, q_li, seg, part, totals, poles, residues, skip_li, near_count):
    tok_rows, channels = z_two.shape
    modes = poles.shape[0]
    column = lambda rows: pl.BlockSpec((rows, LANES), lambda i: (0, i))
    return pl.pallas_call(
        lambda *refs: close_kernel(near_count, *refs),
        grid=(channels // LANES,),
        in_specs=[
            pl.BlockSpec(memory_space=pltpu.SMEM),
            column(tok_rows),
            column(tok_rows),
            column(modes * SEGMENTS),
            column(modes),
            pl.BlockSpec((totals.shape[0], modes, LANES), lambda i: (0, 0, i)),
            column(modes),
            column(modes),
            column(1),
        ],
        out_specs=column(tok_rows),
        out_shape=jax.ShapeDtypeStruct((tok_rows, channels), bf16),
        scratch_shapes=[
            pltpu.VMEM((modes * SEGMENTS, LANES), f32),
            pltpu.VMEM((tok_rows, LANES), f32),
        ],
        compiler_params=small(60.15),
        name="close",
    )(place, z_two, q_li, seg, part, totals, poles, residues, skip_li.reshape(1, channels))


def project_kernel(place_ref, own_ref, other_ref, w_ref, residual_ref, out_ref, y_buf, w_buf, y_sems, w_sems):
    count = own_ref.shape[0]
    copies = []
    for half, y_ref in enumerate((own_ref, other_ref)):
        core = place_ref[1] if half == 0 else 1 - place_ref[1]
        for k in range(count):
            chip = (place_ref[0] + ORDER[k] + count) % count
            i = half * count + k
            copies.append(
                (
                    pltpu.make_async_copy(y_ref.at[k], y_buf.at[i], y_sems.at[i]),
                    pltpu.make_async_copy(w_ref.at[chip, core], w_buf.at[i], w_sems.at[i]),
                )
            )
    for pair in copies:
        for copy in pair:
            copy.start()
    total = residual_ref[...].astype(f32)
    for i, pair in enumerate(copies):
        for copy in pair:
            copy.wait()
        total += jnp.dot(y_buf[i], w_buf[i], preferred_element_type=f32)
    out_ref[...] = total.astype(bf16)


def project(place, own, other, w_all, residual):
    count, tok_rows, depth = own.shape
    columns = w_all.shape[1]
    vmem = pl.BlockSpec(memory_space=pltpu.VMEM)
    hbm = pl.BlockSpec(memory_space=pltpu.HBM)
    arrays = [
        pltpu.with_memory_space_constraint(value, pltpu.HBM)
        for value in (own, other, w_all.reshape(count, 2, depth, columns))
    ]
    return pl.pallas_call(
        project_kernel,
        in_specs=[pl.BlockSpec(memory_space=pltpu.SMEM), hbm, hbm, hbm, vmem],
        out_specs=vmem,
        out_shape=jax.ShapeDtypeStruct((tok_rows, columns), bf16),
        scratch_shapes=[
            pltpu.VMEM((2 * count, tok_rows, depth), bf16),
            pltpu.VMEM((2 * count, depth, columns), bf16),
            pltpu.SemaphoreType.DMA((2 * count,)),
            pltpu.SemaphoreType.DMA((2 * count,)),
        ],
        cost_estimate=pl.CostEstimate(
            flops=4 * count * tok_rows * depth * columns,
            bytes_accessed=4 * count * depth * (tok_rows + columns),
            transcendentals=0,
        ),
        compiler_params=small(20),
        name="project",
    )(place, *arrays, residual)


def tail_kernel(feat_ref, gate_ref, out_ref, sems):
    tok_rows = feat_ref.shape[1]
    at, copies = 0, []
    for ref, stream, rows in (
        (feat_ref, 1, FRONT),
        (feat_ref, 2, FRONT),
        (feat_ref, 0, REACH),
        (gate_ref, 0, REACH),
        (gate_ref, 1, REACH),
    ):
        source = ref.at[stream, pl.ds(tok_rows - rows, rows)]
        copies.append(pltpu.make_async_copy(source, out_ref.at[pl.ds(at, rows)], sems.at[len(copies)]))
        at += rows
    for copy in copies:
        copy.start()
    for copy in copies:
        copy.wait()


def tails(features, gates):
    return pl.pallas_call(
        tail_kernel,
        in_specs=[pl.BlockSpec(memory_space=pltpu.HBM)] * 2,
        out_specs=pl.BlockSpec(memory_space=pltpu.VMEM),
        out_shape=pltpu.VMEM((2 * FRONT + 3 * REACH, features.shape[2]), bf16),
        scratch_shapes=[pltpu.SemaphoreType.DMA((5,))],
        compiler_params=small(60.15),
        name="tails",
    )(features, gates)


ORDER = (0, 1, -1, 2, -2, 3, -3, 4)
NEAR = 4


def on_device(
    residual_in, features, short_mr, medium, skip_mr, li_gates, short_li, poles, residues, skip_li, w_out,
):
    seq_count, tp_count = lax.axis_size("seq"), lax.axis_size("tp")
    rows_count = seq_count // NEAR
    tok_rows = features.shape[1]
    seq_at, tp_at = lax.axis_index("seq"), lax.axis_index("tp")
    place = jnp.stack([seq_at // NEAR, seq_at % NEAR]).astype(jnp.int32)

    w_all = lax.all_gather(w_out, "seq", axis=0, tiled=True)

    tail = tails(features, li_gates)
    halo = lax.ppermute(tail, "seq", [(i, i + 1) for i in range(seq_count - 1)])
    bands = make_bands(medium)
    z_two, q_li, seg, ends = mix(
        features, li_gates, halo, short_mr, short_li, skip_mr, bands, poles, NEAR
    )
    near_groups = [[row * NEAR + i for i in range(NEAR)] for row in range(rows_count)]
    far_groups = [[row * NEAR + i for row in range(rows_count)] for i in range(NEAR)]
    ends = lax.all_to_all(ends, "seq", 0, 0, tiled=True, axis_index_groups=near_groups)
    part, total = near(place, ends, poles, tok_rows, rows_count)
    totals = lax.all_to_all(total, "seq", 0, 0, tiled=True, axis_index_groups=far_groups)
    y_two = close(place, z_two, q_li, seg, part, totals, poles, residues, skip_li, NEAR)

    up = [((t + 2) % tp_count, t) for t in range(tp_count)]
    down = [((t - 2) % tp_count, t) for t in range(tp_count)]
    ahead, behind = y_two, y_two
    pieces = {0: y_two}
    for step in range(1, tp_count // 4 + 1):
        ahead = lax.ppermute(ahead, "tp", up)
        pieces[step] = ahead
        if step < tp_count // 4:
            behind = lax.ppermute(behind, "tp", down)
            pieces[-step] = behind
    own = jnp.stack([pieces[k] for k in ORDER])
    other = lax.ppermute(own, "tp", [(t, t ^ 1) for t in range(tp_count)])
    here = jnp.stack([tp_at // 2, tp_at % 2]).astype(jnp.int32)
    return project(here, own, other, w_all, residual_in)


def solution(mesh):
    placed = (
        P("seq", "tp"),
        P(None, "seq", "tp"),
        P(None, None, "tp"),
        P(None, "tp"),
        P("tp"),
        P(None, "seq", "tp"),
        P(None, None, "tp"),
        P(None, "tp"),
        P(None, "tp"),
        P("tp"),
        P("seq", "tp"),
    )
    return jax.shard_map(
        on_device, mesh=mesh, in_specs=placed, out_specs=P("seq", "tp"), check_vma=False
    )
```

```python
import jax
import jax.numpy as jnp
from jax import lax
from jax.experimental import pallas as pl
from jax.experimental.pallas import tpu as pltpu
from jax.sharding import PartitionSpec as P

f32 = jnp.float32
bf16 = jnp.bfloat16
LANES = 128
SEGMENTS = 8
FRONT = 144
REACH = 16


def small(mebibytes):
    return pltpu.CompilerParams(vmem_limit_bytes=int(mebibytes * 1024) * 1024)


def power(base, exponent):
    result, square = None, base
    while exponent:
        if exponent & 1:
            result = square if result is None else result * square
        exponent >>= 1
        if exponent:
            square = square * square
    return result


def bands_kernel(line_ref, out_ref):
    for group in range(out_ref.shape[0]):
        rows = jnp.broadcast_to(line_ref[group : group + 1, :], out_ref.shape[1:])
        out_ref[group] = pltpu.roll(rows, 0, 1, stride=1, stride_axis=0).astype(bf16)


def make_bands(medium):
    taps, groups = medium.shape
    line = jnp.concatenate(
        [jnp.zeros((1, groups), medium.dtype), medium[::-1], jnp.zeros((taps - 1, groups), medium.dtype)]
    )
    per_step = 8
    return pl.pallas_call(
        bands_kernel,
        grid=(groups // per_step,),
        in_specs=[pl.BlockSpec((per_step, 2 * taps), lambda i: (i, 0))],
        out_specs=pl.BlockSpec((per_step, taps, 2 * taps), lambda i: (i, 0, 0)),
        out_shape=jax.ShapeDtypeStruct((groups, taps, 2 * taps), bf16),
        compiler_params=small(8),
        name="bands",
    )(line.T.astype(f32))


def conv_rows(buffer, taps, first, count):
    total = None
    for lag in range(len(taps)):
        term = taps[lag] * buffer[pl.ds(first - lag, count), :]
        total = term if total is None else total + term
    return total


def mix_kernel(
    feat_ref, gate_ref, halo_ref, short_mr_ref, short_li_ref, skip_ref, band_ref, pole_ref,
    z_ref, q_ref, seg_ref, end_ref,
    k_buf, v_buf, s_buf, y_buf, zwin, state_buf, med_buf,
):
    tok_rows = feat_ref.shape[1]
    taps_med = band_ref.shape[1]
    groups = band_ref.shape[0]
    group_width = LANES // groups
    n_short = short_mr_ref.shape[1]
    step = 32

    def taps_of(ref, stream):
        return [ref[stream, lag : lag + 1, :] for lag in range(n_short)]

    for buf, at, stream in ((k_buf, 0, 1), (v_buf, FRONT, 2)):
        buf[0:8, :] = jnp.zeros((8, LANES), f32)
        buf[8 : 8 + FRONT, :] = halo_ref[at : at + FRONT, :].astype(f32)
        buf[8 + FRONT :, :] = feat_ref[stream].astype(f32)
    k_taps, v_taps = taps_of(short_mr_ref, 1), taps_of(short_mr_ref, 2)
    lead = 2 * taps_med - FRONT
    zwin[0:lead, :] = jnp.zeros((lead, LANES), bf16)
    for first in range(0, FRONT + tok_rows, 16):
        count = 16
        k_part = conv_rows(k_buf, k_taps, 8 + first, count)
        v_part = conv_rows(v_buf, v_taps, 8 + first, count)
        zwin[lead + first : lead + first + count, :] = (k_part * v_part).astype(bf16)

    owner = lax.broadcasted_iota(jnp.int32, (8, LANES), 1) // group_width
    masks = [owner == group for group in range(groups)]

    def pick(product, rows, start):
        for r in range(0, rows, 8):
            total = product[r : r + 8]
            for group in range(1, groups):
                total = jnp.where(masks[group], product[group * rows + r : group * rows + r + 8], total)
            med_buf[start + r : start + r + 8, :] = total

    tail = band_ref[:, taps_med - 16 :, :].reshape(groups * 16, 2 * taps_med)
    pick(jnp.dot(tail, zwin[0 : 2 * taps_med, :], preferred_element_type=f32), 16, 0)
    whole = band_ref[...].reshape(groups * taps_med, 2 * taps_med)
    for block in range(tok_rows // taps_med):
        window = zwin[taps_med * (block + 1) : taps_med * (block + 3), :]
        pick(jnp.dot(whole, window, preferred_element_type=f32), taps_med, 16 + taps_med * block)

    s_buf[0:16, :] = halo_ref[2 * FRONT : 2 * FRONT + 16, :].astype(f32)
    s_buf[16:, :] = feat_ref[0].astype(f32)
    q_taps = taps_of(short_mr_ref, 0)
    skip = skip_ref[...]
    z_last = 2 * taps_med
    q_part = conv_rows(s_buf, q_taps, 8, 8)
    z_part = zwin[z_last - 16 : z_last, :].astype(f32)[8:16]
    y_buf[0:8, :] = (q_part * (med_buf[8:16, :] + skip * z_part)).astype(bf16).astype(f32)
    for first in range(0, tok_rows, step):
        q_part = conv_rows(s_buf, q_taps, 16 + first, step)
        z_part = zwin[z_last + first : z_last + first + step, :].astype(f32)
        y_part = q_part * (med_buf[16 + first : 16 + first + step, :] + skip * z_part)
        y_buf[8 + first : 8 + first + step, :] = y_part.astype(bf16).astype(f32)

    for buf, at, stream in ((k_buf, 16, 0), (v_buf, 32, 1)):
        tail_rows = halo_ref[2 * FRONT + at : 2 * FRONT + at + 16, :].astype(f32)
        buf[0:8, :] = tail_rows[8:16]
        buf[8 : 8 + tok_rows, :] = gate_ref[stream].astype(f32)
    li_taps = [taps_of(short_li_ref, i) for i in range(3)]
    for first in range(0, tok_rows, step):
        rows = slice(first, first + step)
        q_ref[rows, :] = conv_rows(k_buf, li_taps[0], 8 + first, step)
        k_part = conv_rows(v_buf, li_taps[1], 8 + first, step)
        z_ref[rows, :] = k_part * conv_rows(y_buf, li_taps[2], 8 + first, step)

    modes = pole_ref.shape[0]
    seg_rows = tok_rows // SEGMENTS
    pole = [jnp.broadcast_to(pole_ref[m : m + 1, :], (SEGMENTS, LANES)) for m in range(modes)]
    state = [None] * modes
    for t in range(seg_rows):
        z_now = z_ref[pl.ds(t, SEGMENTS, stride=seg_rows), :]
        state = [z_now if s is None else pole[m] * s + z_now for m, s in enumerate(state)]
    for m in range(modes):
        state_buf[m * SEGMENTS : (m + 1) * SEGMENTS, :] = state[m]
    seg_decay = power(pole_ref[...], seg_rows)
    total = state_buf[pl.ds(0, modes, stride=SEGMENTS), :]
    for s in range(1, SEGMENTS):
        total = seg_decay * total + state_buf[pl.ds(s, modes, stride=SEGMENTS), :]
    seg_ref[...] = state_buf[...]
    for copy in range(end_ref.shape[0]):
        end_ref[copy] = total


def mix(features, gates, halo, short_mr, short_li, skip_mr, bands, poles, copies):
    tok_rows, channels = features.shape[1:]
    modes = poles.shape[0]
    groups = bands.shape[0]
    tiles = channels // LANES
    per_tile = groups // tiles
    taps_med = bands.shape[1]
    shapes = [
        ((tok_rows, channels), (tok_rows, LANES), lambda i: (0, i)),
        ((tok_rows, channels), (tok_rows, LANES), lambda i: (0, i)),
        ((modes * SEGMENTS, channels), (modes * SEGMENTS, LANES), lambda i: (0, i)),
        ((copies, modes, channels), (copies, modes, LANES), lambda i: (0, 0, i)),
    ]
    return pl.pallas_call(
        mix_kernel,
        grid=(tiles,),
        in_specs=[
            pl.BlockSpec((3, tok_rows, LANES), lambda i: (0, 0, i)),
            pl.BlockSpec((2, tok_rows, LANES), lambda i: (0, 0, i)),
            pl.BlockSpec((halo.shape[0], LANES), lambda i: (0, i)),
            pl.BlockSpec((3, short_mr.shape[1], LANES), lambda i: (0, 0, i)),
            pl.BlockSpec((3, short_li.shape[1], LANES), lambda i: (0, 0, i)),
            pl.BlockSpec((1, LANES), lambda i: (0, i)),
            pl.BlockSpec((per_tile, taps_med, 2 * taps_med), lambda i: (i, 0, 0)),
            pl.BlockSpec((modes, LANES), lambda i: (0, i)),
        ],
        out_specs=[pl.BlockSpec(block, index) for _, block, index in shapes],
        out_shape=[pltpu.HBM(shape, f32) for shape, _, _ in shapes],
        scratch_shapes=[
            pltpu.VMEM((8 + FRONT + tok_rows, LANES), f32),
            pltpu.VMEM((8 + FRONT + tok_rows, LANES), f32),
            pltpu.VMEM((16 + tok_rows, LANES), f32),
            pltpu.VMEM((8 + tok_rows, LANES), f32),
            pltpu.VMEM((2 * taps_med + tok_rows, LANES), bf16),
            pltpu.VMEM((modes * SEGMENTS, LANES), f32),
            pltpu.VMEM((16 + tok_rows, LANES), f32),
        ],
        compiler_params=small(16),
        name="mix",
    )(features, gates, halo, short_mr, short_li, skip_mr.reshape(1, channels), bands, poles)


def near_kernel(tok_rows, place_ref, ends_ref, pole_ref, part_ref, total_ref):
    mine = place_ref[1]
    decay = power(pole_ref[...], tok_rows)
    part = jnp.zeros(decay.shape, f32)
    total = jnp.zeros(decay.shape, f32)
    for other in range(ends_ref.shape[0]):
        end = ends_ref[other]
        part = jnp.where(other < mine, decay * part + end, part)
        total = decay * total + end
    part_ref[...] = part
    for copy in range(total_ref.shape[0]):
        total_ref[copy] = total


def near(place, ends, poles, tok_rows, copies):
    return pl.pallas_call(
        lambda *refs: near_kernel(tok_rows, *refs),
        in_specs=[
            pl.BlockSpec(memory_space=pltpu.SMEM),
            pl.BlockSpec(memory_space=pltpu.VMEM),
            pl.BlockSpec(memory_space=pltpu.VMEM),
        ],
        out_shape=[
            jax.ShapeDtypeStruct(poles.shape, f32),
            jax.ShapeDtypeStruct((copies, *poles.shape), f32),
        ],
        compiler_params=small(4),
        name="near",
    )(place, ends, poles)


def close_kernel(
    near_count, place_ref, z_ref, q_ref, seg_ref, part_ref, total_ref, pole_ref, res_ref, skip_ref,
    y_ref, state_buf, out_buf,
):
    tok_rows = z_ref.shape[0]
    modes = pole_ref.shape[0]
    seg_rows = tok_rows // SEGMENTS
    row, mine = place_ref[0], place_ref[1]
    seg_decay = power(pole_ref[...], seg_rows)
    decay = power(seg_decay, SEGMENTS)
    row_decay = power(decay, near_count)
    far = jnp.zeros(decay.shape, f32)
    for other in range(total_ref.shape[0]):
        far = jnp.where(other < row, row_decay * far + total_ref[other], far)
    for step in range(near_count - 1):
        far = jnp.where(step < mine, decay * far, far)
    start = far + part_ref[...]
    for s in range(SEGMENTS):
        state_buf[pl.ds(s, modes, stride=SEGMENTS), :] = start
        if s < SEGMENTS - 1:
            start = seg_decay * start + seg_ref[pl.ds(s, modes, stride=SEGMENTS), :]
    state = [state_buf[m * SEGMENTS : (m + 1) * SEGMENTS, :] for m in range(modes)]
    pole = [jnp.broadcast_to(pole_ref[m : m + 1, :], (SEGMENTS, LANES)) for m in range(modes)]
    gain = [jnp.broadcast_to(res_ref[m : m + 1, :], (SEGMENTS, LANES)) for m in range(modes)]
    skip = jnp.broadcast_to(skip_ref[...], (SEGMENTS, LANES))
    for t in range(seg_rows):
        rows = pl.ds(t, SEGMENTS, stride=seg_rows)
        z_now = z_ref[rows, :]
        sums = [skip * z_now, None, None, None]
        for m in range(modes):
            state[m] = pole[m] * state[m] + z_now
            term = gain[m] * state[m]
            sums[m % 4] = term if sums[m % 4] is None else sums[m % 4] + term
        out_buf[rows, :] = q_ref[rows, :] * ((sums[0] + sums[1]) + (sums[2] + sums[3]))
    y_ref[...] = out_buf[...].astype(bf16)


def close(place, z_two, q_li, seg, part, totals, poles, residues, skip_li, near_count):
    tok_rows, channels = z_two.shape
    modes = poles.shape[0]
    column = lambda rows: pl.BlockSpec((rows, LANES), lambda i: (0, i))
    return pl.pallas_call(
        lambda *refs: close_kernel(near_count, *refs),
        grid=(channels // LANES,),
        in_specs=[
            pl.BlockSpec(memory_space=pltpu.SMEM),
            column(tok_rows),
            column(tok_rows),
            column(modes * SEGMENTS),
            column(modes),
            pl.BlockSpec((totals.shape[0], modes, LANES), lambda i: (0, 0, i)),
            column(modes),
            column(modes),
            column(1),
        ],
        out_specs=column(tok_rows),
        out_shape=jax.ShapeDtypeStruct((tok_rows, channels), bf16),
        scratch_shapes=[
            pltpu.VMEM((modes * SEGMENTS, LANES), f32),
            pltpu.VMEM((tok_rows, LANES), f32),
        ],
        compiler_params=small(60.15),
        name="close",
    )(place, z_two, q_li, seg, part, totals, poles, residues, skip_li.reshape(1, channels))


def project_kernel(place_ref, own_ref, other_ref, w_ref, residual_ref, out_ref, y_buf, w_buf, y_sems, w_sems):
    count, _, depth = own_ref.shape
    mine = pl.multiple_of(place_ref[1] * depth, depth)
    theirs = pl.multiple_of((1 - place_ref[1]) * depth, depth)
    copies = []
    for k in range(count):
        chip = (place_ref[0] + ORDER[k] + count) % count
        copies.append(
            (
                pltpu.make_async_copy(own_ref.at[k], y_buf.at[k, :, pl.ds(mine, depth)], y_sems.at[k]),
                pltpu.make_async_copy(other_ref.at[k], y_buf.at[k, :, pl.ds(theirs, depth)], y_sems.at[count + k]),
                pltpu.make_async_copy(w_ref.at[chip], w_buf.at[k], w_sems.at[k]),
            )
        )
    for group in copies:
        for copy in group:
            copy.start()
    total = residual_ref[...].astype(f32)
    for k, group in enumerate(copies):
        for copy in group:
            copy.wait()
        total += jnp.dot(y_buf[k], w_buf[k], preferred_element_type=f32)
    out_ref[...] = total.astype(bf16)


def project(place, own, other, w_all, residual):
    count, tok_rows, depth = own.shape
    columns = w_all.shape[1]
    vmem = pl.BlockSpec(memory_space=pltpu.VMEM)
    hbm = pl.BlockSpec(memory_space=pltpu.HBM)
    arrays = [
        pltpu.with_memory_space_constraint(value, pltpu.HBM)
        for value in (own, other, w_all.reshape(count, 2 * depth, columns))
    ]
    return pl.pallas_call(
        project_kernel,
        in_specs=[pl.BlockSpec(memory_space=pltpu.SMEM), hbm, hbm, hbm, vmem],
        out_specs=vmem,
        out_shape=jax.ShapeDtypeStruct((tok_rows, columns), bf16),
        scratch_shapes=[
            pltpu.VMEM((count, tok_rows, 2 * depth), bf16),
            pltpu.VMEM((count, 2 * depth, columns), bf16),
            pltpu.SemaphoreType.DMA((2 * count,)),
            pltpu.SemaphoreType.DMA((count,)),
        ],
        cost_estimate=pl.CostEstimate(
            flops=4 * count * tok_rows * depth * columns,
            bytes_accessed=4 * count * depth * (tok_rows + columns),
            transcendentals=0,
        ),
        compiler_params=small(20),
        name="project",
    )(place, *arrays, residual)


def tail_kernel(feat_ref, gate_ref, out_ref, sems):
    tok_rows = feat_ref.shape[1]
    at, copies = 0, []
    for ref, stream, rows in (
        (feat_ref, 1, FRONT),
        (feat_ref, 2, FRONT),
        (feat_ref, 0, REACH),
        (gate_ref, 0, REACH),
        (gate_ref, 1, REACH),
    ):
        source = ref.at[stream, pl.ds(tok_rows - rows, rows)]
        copies.append(pltpu.make_async_copy(source, out_ref.at[pl.ds(at, rows)], sems.at[len(copies)]))
        at += rows
    for copy in copies:
        copy.start()
    for copy in copies:
        copy.wait()


def tails(features, gates):
    return pl.pallas_call(
        tail_kernel,
        in_specs=[pl.BlockSpec(memory_space=pltpu.HBM)] * 2,
        out_specs=pl.BlockSpec(memory_space=pltpu.VMEM),
        out_shape=pltpu.VMEM((2 * FRONT + 3 * REACH, features.shape[2]), bf16),
        scratch_shapes=[pltpu.SemaphoreType.DMA((5,))],
        compiler_params=small(60.15),
        name="tails",
    )(features, gates)


ORDER = (0, 1, -1, 2, -2, 3, -3, 4)
NEAR = 4


def on_device(
    residual_in, features, short_mr, medium, skip_mr, li_gates, short_li, poles, residues, skip_li, w_out,
):
    seq_count, tp_count = lax.axis_size("seq"), lax.axis_size("tp")
    rows_count = seq_count // NEAR
    tok_rows = features.shape[1]
    seq_at, tp_at = lax.axis_index("seq"), lax.axis_index("tp")
    place = jnp.stack([seq_at // NEAR, seq_at % NEAR]).astype(jnp.int32)

    w_all = lax.all_gather(w_out, "seq", axis=0, tiled=True)

    tail = tails(features, li_gates)
    halo = lax.ppermute(tail, "seq", [(i, i + 1) for i in range(seq_count - 1)])
    bands = make_bands(medium)
    z_two, q_li, seg, ends = mix(
        features, li_gates, halo, short_mr, short_li, skip_mr, bands, poles, NEAR
    )
    near_groups = [[row * NEAR + i for i in range(NEAR)] for row in range(rows_count)]
    far_groups = [[row * NEAR + i for row in range(rows_count)] for i in range(NEAR)]
    ends = lax.all_to_all(ends, "seq", 0, 0, tiled=True, axis_index_groups=near_groups)
    part, total = near(place, ends, poles, tok_rows, rows_count)
    totals = lax.all_to_all(total, "seq", 0, 0, tiled=True, axis_index_groups=far_groups)
    y_two = close(place, z_two, q_li, seg, part, totals, poles, residues, skip_li, NEAR)

    up = [((t + 2) % tp_count, t) for t in range(tp_count)]
    down = [((t - 2) % tp_count, t) for t in range(tp_count)]
    ahead, behind = y_two, y_two
    pieces = {0: y_two}
    for step in range(1, tp_count // 4 + 1):
        ahead = lax.ppermute(ahead, "tp", up)
        pieces[step] = ahead
        if step < tp_count // 4:
            behind = lax.ppermute(behind, "tp", down)
            pieces[-step] = behind
    own = jnp.stack([pieces[k] for k in ORDER])
    other = lax.ppermute(own, "tp", [(t, t ^ 1) for t in range(tp_count)])
    here = jnp.stack([tp_at // 2, tp_at % 2]).astype(jnp.int32)
    return project(here, own, other, w_all, residual_in)


def solution(mesh):
    placed = (
        P("seq", "tp"),
        P(None, "seq", "tp"),
        P(None, None, "tp"),
        P(None, "tp"),
        P("tp"),
        P(None, "seq", "tp"),
        P(None, None, "tp"),
        P(None, "tp"),
        P(None, "tp"),
        P("tp"),
        P("seq", "tp"),
    )
    return jax.shard_map(
        on_device, mesh=mesh, in_specs=placed, out_specs=P("seq", "tp"), check_vma=False
    )
```

```python
import jax
import jax.numpy as jnp
from jax import lax
from jax.experimental import pallas as pl
from jax.experimental.pallas import tpu as pltpu
from jax.sharding import PartitionSpec as P

f32 = jnp.float32
bf16 = jnp.bfloat16
LANES = 128
SEGMENTS = 8
FRONT = 144
REACH = 16


def small(mebibytes):
    return pltpu.CompilerParams(vmem_limit_bytes=int(mebibytes * 1024) * 1024)


def power(base, exponent):
    result, square = None, base
    while exponent:
        if exponent & 1:
            result = square if result is None else result * square
        exponent >>= 1
        if exponent:
            square = square * square
    return result


def bands_kernel(line_ref, out_ref):
    for group in range(out_ref.shape[0]):
        rows = jnp.broadcast_to(line_ref[group : group + 1, :], out_ref.shape[1:])
        out_ref[group] = pltpu.roll(rows, 0, 1, stride=1, stride_axis=0).astype(bf16)


def make_bands(medium):
    taps, groups = medium.shape
    line = jnp.concatenate(
        [jnp.zeros((1, groups), medium.dtype), medium[::-1], jnp.zeros((taps - 1, groups), medium.dtype)]
    )
    per_step = 8
    return pl.pallas_call(
        bands_kernel,
        grid=(groups // per_step,),
        in_specs=[pl.BlockSpec((per_step, 2 * taps), lambda i: (i, 0))],
        out_specs=pl.BlockSpec((per_step, taps, 2 * taps), lambda i: (i, 0, 0)),
        out_shape=jax.ShapeDtypeStruct((groups, taps, 2 * taps), bf16),
        compiler_params=small(8),
        name="bands",
    )(line.T.astype(f32))


def conv_rows(buffer, taps, first, count):
    total = None
    for lag in range(len(taps)):
        term = taps[lag] * buffer[pl.ds(first - lag, count), :]
        total = term if total is None else total + term
    return total


def mix_kernel(
    feat_ref, gate_ref, halo_ref, short_mr_ref, short_li_ref, skip_ref, band_ref, pole_ref,
    z_ref, q_ref, seg_ref, end_ref,
    k_buf, v_buf, s_buf, y_buf, zwin, state_buf, med_buf,
):
    tok_rows = feat_ref.shape[1]
    taps_med = band_ref.shape[1]
    groups = band_ref.shape[0]
    group_width = LANES // groups
    n_short = short_mr_ref.shape[1]
    step = 32

    def taps_of(ref, stream):
        return [ref[stream, lag : lag + 1, :] for lag in range(n_short)]

    for buf, at, stream in ((k_buf, 0, 1), (v_buf, FRONT, 2)):
        buf[0:8, :] = jnp.zeros((8, LANES), f32)
        buf[8 : 8 + FRONT, :] = halo_ref[at : at + FRONT, :].astype(f32)
        buf[8 + FRONT :, :] = feat_ref[stream].astype(f32)
    k_taps, v_taps = taps_of(short_mr_ref, 1), taps_of(short_mr_ref, 2)
    lead = 2 * taps_med - FRONT
    zwin[0:lead, :] = jnp.zeros((lead, LANES), bf16)
    for first in range(0, FRONT + tok_rows, 16):
        count = 16
        k_part = conv_rows(k_buf, k_taps, 8 + first, count)
        v_part = conv_rows(v_buf, v_taps, 8 + first, count)
        zwin[lead + first : lead + first + count, :] = (k_part * v_part).astype(bf16)

    owner = lax.broadcasted_iota(jnp.int32, (8, LANES), 1) // group_width
    masks = [owner == group for group in range(groups)]

    def pick(product, rows, start):
        for r in range(0, rows, 8):
            total = product[r : r + 8]
            for group in range(1, groups):
                total = jnp.where(masks[group], product[group * rows + r : group * rows + r + 8], total)
            med_buf[start + r : start + r + 8, :] = total

    tail = band_ref[:, taps_med - 16 :, :].reshape(groups * 16, 2 * taps_med)
    pick(jnp.dot(tail, zwin[0 : 2 * taps_med, :], preferred_element_type=f32), 16, 0)
    whole = band_ref[...].reshape(groups * taps_med, 2 * taps_med)
    for block in range(tok_rows // taps_med):
        window = zwin[taps_med * (block + 1) : taps_med * (block + 3), :]
        pick(jnp.dot(whole, window, preferred_element_type=f32), taps_med, 16 + taps_med * block)

    s_buf[0:16, :] = halo_ref[2 * FRONT : 2 * FRONT + 16, :].astype(f32)
    s_buf[16:, :] = feat_ref[0].astype(f32)
    q_taps = taps_of(short_mr_ref, 0)
    skip = skip_ref[...]
    z_last = 2 * taps_med
    q_part = conv_rows(s_buf, q_taps, 8, 8)
    z_part = zwin[z_last - 16 : z_last, :].astype(f32)[8:16]
    y_buf[0:8, :] = (q_part * (med_buf[8:16, :] + skip * z_part)).astype(bf16).astype(f32)
    for first in range(0, tok_rows, step):
        q_part = conv_rows(s_buf, q_taps, 16 + first, step)
        z_part = zwin[z_last + first : z_last + first + step, :].astype(f32)
        y_part = q_part * (med_buf[16 + first : 16 + first + step, :] + skip * z_part)
        y_buf[8 + first : 8 + first + step, :] = y_part.astype(bf16).astype(f32)

    for buf, at, stream in ((k_buf, 16, 0), (v_buf, 32, 1)):
        tail_rows = halo_ref[2 * FRONT + at : 2 * FRONT + at + 16, :].astype(f32)
        buf[0:8, :] = tail_rows[8:16]
        buf[8 : 8 + tok_rows, :] = gate_ref[stream].astype(f32)
    li_taps = [taps_of(short_li_ref, i) for i in range(3)]
    for first in range(0, tok_rows, step):
        rows = slice(first, first + step)
        q_ref[rows, :] = conv_rows(k_buf, li_taps[0], 8 + first, step)
        k_part = conv_rows(v_buf, li_taps[1], 8 + first, step)
        z_ref[rows, :] = k_part * conv_rows(y_buf, li_taps[2], 8 + first, step)

    modes = pole_ref.shape[0]
    seg_rows = tok_rows // SEGMENTS
    pole = [jnp.broadcast_to(pole_ref[m : m + 1, :], (SEGMENTS, LANES)) for m in range(modes)]
    state = [None] * modes
    for t in range(seg_rows):
        z_now = z_ref[pl.ds(t, SEGMENTS, stride=seg_rows), :]
        state = [z_now if s is None else pole[m] * s + z_now for m, s in enumerate(state)]
    for m in range(modes):
        state_buf[m * SEGMENTS : (m + 1) * SEGMENTS, :] = state[m]
    seg_decay = power(pole_ref[...], seg_rows)
    total = state_buf[pl.ds(0, modes, stride=SEGMENTS), :]
    for s in range(1, SEGMENTS):
        total = seg_decay * total + state_buf[pl.ds(s, modes, stride=SEGMENTS), :]
    seg_ref[...] = state_buf[...]
    for copy in range(end_ref.shape[0]):
        end_ref[copy] = total


def mix(features, gates, halo, short_mr, short_li, skip_mr, bands, poles, copies):
    tok_rows, channels = features.shape[1:]
    modes = poles.shape[0]
    groups = bands.shape[0]
    tiles = channels // LANES
    per_tile = groups // tiles
    taps_med = bands.shape[1]
    shapes = [
        ((tok_rows, channels), (tok_rows, LANES), lambda i: (0, i)),
        ((tok_rows, channels), (tok_rows, LANES), lambda i: (0, i)),
        ((modes * SEGMENTS, channels), (modes * SEGMENTS, LANES), lambda i: (0, i)),
        ((copies, modes, channels), (copies, modes, LANES), lambda i: (0, 0, i)),
    ]
    return pl.pallas_call(
        mix_kernel,
        grid=(tiles,),
        in_specs=[
            pl.BlockSpec((3, tok_rows, LANES), lambda i: (0, 0, i)),
            pl.BlockSpec((2, tok_rows, LANES), lambda i: (0, 0, i)),
            pl.BlockSpec((halo.shape[0], LANES), lambda i: (0, i)),
            pl.BlockSpec((3, short_mr.shape[1], LANES), lambda i: (0, 0, i)),
            pl.BlockSpec((3, short_li.shape[1], LANES), lambda i: (0, 0, i)),
            pl.BlockSpec((1, LANES), lambda i: (0, i)),
            pl.BlockSpec((per_tile, taps_med, 2 * taps_med), lambda i: (i, 0, 0)),
            pl.BlockSpec((modes, LANES), lambda i: (0, i)),
        ],
        out_specs=[pl.BlockSpec(block, index) for _, block, index in shapes],
        out_shape=[pltpu.HBM(shape, f32) for shape, _, _ in shapes],
        scratch_shapes=[
            pltpu.VMEM((8 + FRONT + tok_rows, LANES), f32),
            pltpu.VMEM((8 + FRONT + tok_rows, LANES), f32),
            pltpu.VMEM((16 + tok_rows, LANES), f32),
            pltpu.VMEM((8 + tok_rows, LANES), f32),
            pltpu.VMEM((2 * taps_med + tok_rows, LANES), bf16),
            pltpu.VMEM((modes * SEGMENTS, LANES), f32),
            pltpu.VMEM((16 + tok_rows, LANES), f32),
        ],
        compiler_params=small(16),
        name="mix",
    )(features, gates, halo, short_mr, short_li, skip_mr.reshape(1, channels), bands, poles)


def near_kernel(tok_rows, place_ref, ends_ref, pole_ref, part_ref, total_ref):
    mine = place_ref[1]
    decay = power(pole_ref[...], tok_rows)
    part = jnp.zeros(decay.shape, f32)
    total = jnp.zeros(decay.shape, f32)
    for other in range(ends_ref.shape[0]):
        end = ends_ref[other]
        part = jnp.where(other < mine, decay * part + end, part)
        total = decay * total + end
    part_ref[...] = part
    for copy in range(total_ref.shape[0]):
        total_ref[copy] = total


def near(place, ends, poles, tok_rows, copies):
    return pl.pallas_call(
        lambda *refs: near_kernel(tok_rows, *refs),
        in_specs=[
            pl.BlockSpec(memory_space=pltpu.SMEM),
            pl.BlockSpec(memory_space=pltpu.VMEM),
            pl.BlockSpec(memory_space=pltpu.VMEM),
        ],
        out_shape=[
            jax.ShapeDtypeStruct(poles.shape, f32),
            jax.ShapeDtypeStruct((copies, *poles.shape), f32),
        ],
        compiler_params=small(4),
        name="near",
    )(place, ends, poles)


def close_kernel(
    near_count, place_ref, z_ref, q_ref, seg_ref, part_ref, total_ref, pole_ref, res_ref, skip_ref,
    y_ref, state_buf, out_buf,
):
    tok_rows = z_ref.shape[0]
    modes = pole_ref.shape[0]
    seg_rows = tok_rows // SEGMENTS
    row, mine = place_ref[0], place_ref[1]
    seg_decay = power(pole_ref[...], seg_rows)
    decay = power(seg_decay, SEGMENTS)
    row_decay = power(decay, near_count)
    far = jnp.zeros(decay.shape, f32)
    for other in range(total_ref.shape[0]):
        far = jnp.where(other < row, row_decay * far + total_ref[other], far)
    for step in range(near_count - 1):
        far = jnp.where(step < mine, decay * far, far)
    start = far + part_ref[...]
    for s in range(SEGMENTS):
        state_buf[pl.ds(s, modes, stride=SEGMENTS), :] = start
        if s < SEGMENTS - 1:
            start = seg_decay * start + seg_ref[pl.ds(s, modes, stride=SEGMENTS), :]
    state = [state_buf[m * SEGMENTS : (m + 1) * SEGMENTS, :] for m in range(modes)]
    pole = [jnp.broadcast_to(pole_ref[m : m + 1, :], (SEGMENTS, LANES)) for m in range(modes)]
    gain = [jnp.broadcast_to(res_ref[m : m + 1, :], (SEGMENTS, LANES)) for m in range(modes)]
    skip = jnp.broadcast_to(skip_ref[...], (SEGMENTS, LANES))
    for t in range(seg_rows):
        rows = pl.ds(t, SEGMENTS, stride=seg_rows)
        z_now = z_ref[rows, :]
        sums = [skip * z_now, None, None, None]
        for m in range(modes):
            state[m] = pole[m] * state[m] + z_now
            term = gain[m] * state[m]
            sums[m % 4] = term if sums[m % 4] is None else sums[m % 4] + term
        out_buf[rows, :] = q_ref[rows, :] * ((sums[0] + sums[1]) + (sums[2] + sums[3]))
    y_ref[...] = out_buf[...].astype(bf16)


def close(place, z_two, q_li, seg, part, totals, poles, residues, skip_li, near_count):
    tok_rows, channels = z_two.shape
    modes = poles.shape[0]
    column = lambda rows: pl.BlockSpec((rows, LANES), lambda i: (0, i))
    return pl.pallas_call(
        lambda *refs: close_kernel(near_count, *refs),
        grid=(channels // LANES,),
        in_specs=[
            pl.BlockSpec(memory_space=pltpu.SMEM),
            column(tok_rows),
            column(tok_rows),
            column(modes * SEGMENTS),
            column(modes),
            pl.BlockSpec((totals.shape[0], modes, LANES), lambda i: (0, 0, i)),
            column(modes),
            column(modes),
            column(1),
        ],
        out_specs=column(tok_rows),
        out_shape=jax.ShapeDtypeStruct((tok_rows, channels), bf16),
        scratch_shapes=[
            pltpu.VMEM((modes * SEGMENTS, LANES), f32),
            pltpu.VMEM((tok_rows, LANES), f32),
        ],
        compiler_params=small(60.15),
        name="close",
    )(place, z_two, q_li, seg, part, totals, poles, residues, skip_li.reshape(1, channels))


def project_kernel(place_ref, own_ref, other_ref, w_ref, residual_ref, out_ref, y_buf, w_buf, y_sems, w_sems):
    count, _, depth = own_ref.shape
    mine = pl.multiple_of(place_ref[1] * depth, depth)
    theirs = pl.multiple_of((1 - place_ref[1]) * depth, depth)
    copies = []
    for k in range(count):
        chip = (place_ref[0] + ORDER[k] + count) % count
        copies.append(
            (
                pltpu.make_async_copy(own_ref.at[k], y_buf.at[k, :, pl.ds(mine, depth)], y_sems.at[k]),
                pltpu.make_async_copy(other_ref.at[k], y_buf.at[k, :, pl.ds(theirs, depth)], y_sems.at[count + k]),
                pltpu.make_async_copy(w_ref.at[chip], w_buf.at[k], w_sems.at[k]),
            )
        )
    for group in copies:
        for copy in group[::-1]:
            copy.start()
    total = residual_ref[...].astype(f32)
    for k, group in enumerate(copies):
        for copy in group:
            copy.wait()
        total += jnp.dot(y_buf[k], w_buf[k], preferred_element_type=f32)
    out_ref[...] = total.astype(bf16)


def project(place, own, other, w_all, residual):
    count, tok_rows, depth = own.shape
    columns = w_all.shape[1]
    vmem = pl.BlockSpec(memory_space=pltpu.VMEM)
    hbm = pl.BlockSpec(memory_space=pltpu.HBM)
    arrays = [
        pltpu.with_memory_space_constraint(value, pltpu.HBM)
        for value in (own, other, w_all.reshape(count, 2 * depth, columns))
    ]
    return pl.pallas_call(
        project_kernel,
        in_specs=[pl.BlockSpec(memory_space=pltpu.SMEM), hbm, hbm, hbm, vmem],
        out_specs=vmem,
        out_shape=jax.ShapeDtypeStruct((tok_rows, columns), bf16),
        scratch_shapes=[
            pltpu.VMEM((count, tok_rows, 2 * depth), bf16),
            pltpu.VMEM((count, 2 * depth, columns), bf16),
            pltpu.SemaphoreType.DMA((2 * count,)),
            pltpu.SemaphoreType.DMA((count,)),
        ],
        cost_estimate=pl.CostEstimate(
            flops=4 * count * tok_rows * depth * columns,
            bytes_accessed=4 * count * depth * (tok_rows + columns),
            transcendentals=0,
        ),
        compiler_params=small(20),
        name="project",
    )(place, *arrays, residual)


def tail_kernel(feat_ref, gate_ref, out_ref, sems):
    tok_rows = feat_ref.shape[1]
    at, copies = 0, []
    for ref, stream, rows in (
        (feat_ref, 1, FRONT),
        (feat_ref, 2, FRONT),
        (feat_ref, 0, REACH),
        (gate_ref, 0, REACH),
        (gate_ref, 1, REACH),
    ):
        source = ref.at[stream, pl.ds(tok_rows - rows, rows)]
        copies.append(pltpu.make_async_copy(source, out_ref.at[pl.ds(at, rows)], sems.at[len(copies)]))
        at += rows
    for copy in copies:
        copy.start()
    for copy in copies:
        copy.wait()


def tails(features, gates):
    return pl.pallas_call(
        tail_kernel,
        in_specs=[pl.BlockSpec(memory_space=pltpu.HBM)] * 2,
        out_specs=pl.BlockSpec(memory_space=pltpu.VMEM),
        out_shape=pltpu.VMEM((2 * FRONT + 3 * REACH, features.shape[2]), bf16),
        scratch_shapes=[pltpu.SemaphoreType.DMA((5,))],
        compiler_params=small(60.15),
        name="tails",
    )(features, gates)


ORDER = (0, 1, -1, 2, -2, 3, -3, 4)
NEAR = 4


def on_device(
    residual_in, features, short_mr, medium, skip_mr, li_gates, short_li, poles, residues, skip_li, w_out,
):
    seq_count, tp_count = lax.axis_size("seq"), lax.axis_size("tp")
    rows_count = seq_count // NEAR
    tok_rows = features.shape[1]
    seq_at, tp_at = lax.axis_index("seq"), lax.axis_index("tp")
    place = jnp.stack([seq_at // NEAR, seq_at % NEAR]).astype(jnp.int32)

    w_all = lax.all_gather(w_out, "seq", axis=0, tiled=True)

    tail = tails(features, li_gates)
    halo = lax.ppermute(tail, "seq", [(i, i + 1) for i in range(seq_count - 1)])
    bands = make_bands(medium)
    z_two, q_li, seg, ends = mix(
        features, li_gates, halo, short_mr, short_li, skip_mr, bands, poles, NEAR
    )
    near_groups = [[row * NEAR + i for i in range(NEAR)] for row in range(rows_count)]
    far_groups = [[row * NEAR + i for row in range(rows_count)] for i in range(NEAR)]
    ends = lax.all_to_all(ends, "seq", 0, 0, tiled=True, axis_index_groups=near_groups)
    part, total = near(place, ends, poles, tok_rows, rows_count)
    totals = lax.all_to_all(total, "seq", 0, 0, tiled=True, axis_index_groups=far_groups)
    y_two = close(place, z_two, q_li, seg, part, totals, poles, residues, skip_li, NEAR)

    up = [((t + 2) % tp_count, t) for t in range(tp_count)]
    down = [((t - 2) % tp_count, t) for t in range(tp_count)]
    ahead, behind = y_two, y_two
    pieces = {0: y_two}
    for step in range(1, tp_count // 4 + 1):
        ahead = lax.ppermute(ahead, "tp", up)
        pieces[step] = ahead
        if step < tp_count // 4:
            behind = lax.ppermute(behind, "tp", down)
            pieces[-step] = behind
    own = jnp.stack([pieces[k] for k in ORDER])
    other = lax.ppermute(own, "tp", [(t, t ^ 1) for t in range(tp_count)])
    here = jnp.stack([tp_at // 2, tp_at % 2]).astype(jnp.int32)
    return project(here, own, other, w_all, residual_in)


def solution(mesh):
    placed = (
        P("seq", "tp"),
        P(None, "seq", "tp"),
        P(None, None, "tp"),
        P(None, "tp"),
        P("tp"),
        P(None, "seq", "tp"),
        P(None, None, "tp"),
        P(None, "tp"),
        P(None, "tp"),
        P("tp"),
        P("seq", "tp"),
    )
    return jax.shard_map(
        on_device, mesh=mesh, in_specs=placed, out_specs=P("seq", "tp"), check_vma=False
    )
```
